256 devices in a mesh: group: 8 (over z_lo, core), tensor: 32 (over y, x, z_hi).
Axes of the slice: x: 4, y: 4, z: 8 (z_hi: 2, z_lo: 4; z = z_hi * 4 + z_lo), core: 2. Of those that a mesh axis runs over, the one named last changes fastest.
Arguments:
- grad_a: float32 [8, 16, 64, 4096], P('group', None, None, 'tensor'), may hold values from -6 to 6
- grad_b: float32 [8, 16, 1536, 64], P('group', None, 'tensor'), may hold values from -6 to 6
- factor_a: float32 [16, 64, 4096], P('group', None, 'tensor'), may hold values from -6 to 6
- factor_b: float32 [16, 1536, 64], P('group', 'tensor'), may hold values from -6 to 6
- moment_a: float32 [16, 64, 4096], P('group', None, 'tensor'), may hold values from -6 to 6
- second_a: float32 [16, 64, 4096], P('group', None, 'tensor'), may hold values from 0.01 to 1
- moment_b: float32 [16, 1536, 64], P('group', 'tensor'), may hold values from -6 to 6
- second_b: float32 [16, 1536, 64], P('group', 'tensor'), may hold values from 0.01 to 1
- base_rows: bfloat16 [16, 1536, 4096], P(None, 'tensor'), may hold values from -6 to 6
Outputs:
- new_factor_a: float32 [16, 64, 4096], P('group', None, 'tensor')
- new_factor_b: float32 [16, 1536, 64], P('group', 'tensor')
- new_moment_a: float32 [16, 64, 4096], P('group', None, 'tensor')
- new_second_a: float32 [16, 64, 4096], P('group', None, 'tensor')
- new_moment_b: float32 [16, 1536, 64], P('group', 'tensor')
- new_second_b: float32 [16, 1536, 64], P('group', 'tensor')
- merged: bfloat16 [16, 1536, 4096], P(None, 'tensor')
The draws below stay inside these ranges and needn't reach their ends.
All inputs are finite; a program needn't handle non-finite values.
Results may differ from the reference program's by a relative error of at most 0.011.
Values may be sent and summed in bfloat16 or wider, within the bound.
No kernel may reach another device: no remote copies, remote signals or barrier semaphores. Data moves between devices by JAX's collectives and lax.ppermute only.
A program may use at most 64 MiB of HBM per device.

```python
import math
import jax
import jax.numpy as jnp
from jax import lax

D = 4096
FF = 1536
R = 64
STEP = 100
E = 16
N_GROUP = 8


def raised(array, key, source, target, shards_of, factor):
    owner, partner = [(jnp.arange(array.shape[dim]) // (array.shape[dim] // shards_of)).reshape([-1 if axis == dim else 1 for axis in range(array.ndim)]) for dim in (source, target)]
    chosen = jax.random.permutation(key, shards_of)[partner]
    strong = (owner == chosen) | (owner == (partner + shards_of // 2) % shards_of)
    return jnp.where(strong, factor * array, array)


def levels(stream_key, extent, pieces, smallest, largest):
    def one(dim, blocks):
        heights = jax.random.uniform(jax.random.fold_in(jax.random.fold_in(stream_key, 6), dim), (blocks,), jnp.float32, smallest / len(pieces), largest / len(pieces))
        return jnp.repeat(jnp.exp(heights), extent[dim] // blocks).reshape((-1,) + (1,) * (len(extent) - dim - 1))

    gain = one(*pieces[0])
    for cut in pieces[1:]:
        gain = gain * one(*cut)
    return gain


def centred(own_key, extent, scale, reach, split=(), dtype=jnp.bfloat16):
    entries = scale * jax.random.normal(own_key, extent, jnp.float32)
    if split:
        entries = entries * levels(own_key, extent, split, -0.22, 0.18)
    return jnp.clip(entries, -reach, reach).astype(dtype)


def heavy_noise(stream_key, dims, deviation, most, pieces, heavy, dtype=jnp.bfloat16):
    values = deviation * jax.random.normal(stream_key, dims, jnp.float32)
    if pieces:
        values = values * levels(stream_key, dims, pieces, -0.22, 0.18)
    return jnp.clip(raised(values, jax.random.fold_in(stream_key, 3), *heavy), -most, most).astype(dtype)


def setup_inputs(seed: int = 0) -> dict:
    key_of = jax.random.split(jax.random.key(seed), 10)
    grad_a = heavy_noise(key_of[0], (N_GROUP, E, R, D), 1.0, 6.0, ((0, 8), (3, 32)), (0, 1, 8, 2.0), jnp.float32)
    grad_b = heavy_noise(key_of[1], (N_GROUP, E, FF, R), 1.0, 6.0, ((0, 8), (2, 32)), (0, 1, 8, 2.0), jnp.float32)
    factor_a = centred(key_of[2], (E, R, D), 1.0, 6.0, ((0, 8), (2, 32)), jnp.float32)
    factor_b = centred(key_of[3], (E, FF, R), 1.0, 6.0, ((0, 8), (1, 32)), jnp.float32)
    moment_a = centred(key_of[4], (E, R, D), 0.5, 6.0, ((0, 8), (2, 32)), jnp.float32)
    second_a = jnp.clip(jnp.exp(math.log(1.0) - 4.6051702 * jax.random.uniform(key_of[5], (E, R, D), jnp.float32) ** levels(key_of[5], (E, R, D), ((0, 8), (2, 32)), -0.2, 0.2)), 0.01, 1.0)
    moment_b = centred(key_of[6], (E, FF, R), 0.5, 6.0, ((0, 8), (1, 32)), jnp.float32)
    second_b = jnp.clip(jnp.exp(math.log(1.0) - 4.6051702 * jax.random.uniform(key_of[7], (E, FF, R), jnp.float32) ** levels(key_of[7], (E, FF, R), ((0, 8), (1, 32)), -0.2, 0.2)), 0.01, 1.0)
    base_rows = centred(key_of[8], (E, FF, D), 1.0, 6.0, ((1, 32),))
    return {"grad_a": grad_a, "grad_b": grad_b, "factor_a": factor_a, "factor_b": factor_b, "moment_a": moment_a, "second_a": second_a, "moment_b": moment_b, "second_b": second_b, "base_rows": base_rows}


def adam_update(param, grad, first, second):
    new_first = 0.9 * first + 0.1 * grad
    new_second = 0.999 * second + 0.001 * grad * grad
    corr_first = new_first / (1.0 - 0.9 ** STEP)
    corr_second = new_second / (1.0 - 0.999 ** STEP)
    new_param = param - 0.1 * corr_first / (jnp.sqrt(corr_second) + 1e-08)
    return (new_param, new_first, new_second)

def reference(grad_a, grad_b, factor_a, factor_b, moment_a, second_a, moment_b, second_b, base_rows):
    sum_a = lax.optimization_barrier(jnp.sum(grad_a, axis=0))
    sum_b = lax.optimization_barrier(jnp.sum(grad_b, axis=0))
    new_a, new_ma, new_va = adam_update(factor_a, sum_a, moment_a, second_a)
    new_b, new_mb, new_vb = adam_update(factor_b, sum_b, moment_b, second_b)
    a_half = new_a.astype(jnp.bfloat16)
    b_half = new_b.astype(jnp.bfloat16)

    def merge_one(items):
        b_one, a_one, w_one = items
        delta = jnp.dot(b_one, a_one, preferred_element_type=jnp.float32)
        return (w_one.astype(jnp.float32) + 0.125 * delta).astype(jnp.bfloat16)
    merged = lax.map(merge_one, (b_half, a_half, base_rows))
    return (new_a, new_b, new_ma, new_va, new_mb, new_vb, merged)
```

```python
import jax
import jax.numpy as jnp
from jax import lax
from jax.experimental import pallas as pl
from jax.experimental.pallas import tpu as pltpu
from jax.sharding import Mesh, PartitionSpec as P

STEP = 100
HALF = jnp.bfloat16
VMEM = pl.BlockSpec(memory_space=pltpu.VMEM)


def adam_update(param, grad, first, second):
    new_first = 0.9 * first + 0.1 * grad
    new_second = 0.999 * second + 0.001 * grad * grad
    corr_first = new_first / (1.0 - 0.9**STEP)
    corr_second = new_second / (1.0 - 0.999**STEP)
    new_param = param - 0.1 * corr_first / (jnp.sqrt(corr_second) + 1e-08)
    return (new_param, new_first, new_second)


def pack_kernel(grad_a, grad_b, out):
    out[:, 0:128, :] = grad_a[0].reshape(8, 128, 128).astype(HALF)
    for owner in range(8):
        pair = jnp.concatenate([grad_b[0, 2 * owner], grad_b[0, 2 * owner + 1]], axis=-1)
        out[owner, 128:176, :] = pair.astype(HALF)


def update_kernel(
    got, factor_a, factor_b, moment_a, second_a, moment_b, second_b,
    new_a, new_b, new_ma, new_va, new_mb, new_vb, send,
):
    total = got[0].astype(jnp.float32)
    for learner in range(1, 8):
        total = total + got[learner].astype(jnp.float32)
    grad_a = total[0:128].reshape(2, 64, 128)
    a, ma, va = adam_update(factor_a[...], grad_a, moment_a[...], second_a[...])
    new_a[...] = a
    new_ma[...] = ma
    new_va[...] = va
    halves = []
    for expert in range(2):
        grad_b = total[128:176, 64 * expert : 64 * expert + 64]
        b, mb, vb = adam_update(factor_b[expert], grad_b, moment_b[expert], second_b[expert])
        new_b[expert] = b
        new_mb[expert] = mb
        new_vb[expert] = vb
        halves.append(b)
    a_half = a.astype(HALF).reshape(128, 128)
    b_half = jnp.concatenate(halves, axis=-1).astype(HALF)
    for peer in range(8):
        send[peer, 0:128, :] = a_half
        send[peer, 128:176, :] = b_half


def merge_kernel(place, b_own, b_sibling, base, *rest):
    pieces = rest[:16]
    out, blocks = rest[16:]
    x, core = place[0], place[2]
    ky = pl.program_id(0)

    @pl.when(ky == 0)
    def _():
        blocks[...] = jnp.zeros_like(blocks)
        for side, rows in ((0, b_own), (1, b_sibling)):
            for h in range(2):
                for zl in range(4):
                    blocks[side, h, 48 * zl : 48 * zl + 48, 64 * zl : 64 * zl + 64] = rows[
                        zl, :, 64 * h : 64 * h + 64
                    ]

    def one(step):
        for kx in range(4):
            column = pl.multiple_of(lax.rem(x + 4 - kx, 4) * 256, 256)
            for side in range(2):
                for h in range(2):
                    if h == 0:
                        piece = pieces[8 * side + step][kx]
                    else:
                        piece = pieces[8 * side + 4 + kx][step]
                    wide = jnp.concatenate(
                        [piece[:, 0].reshape(256, 128), piece[:, 1].reshape(256, 128)], axis=-1
                    )
                    delta = jnp.dot(
                        blocks[side, h], wide, preferred_element_type=jnp.float32
                    ).reshape(4, 48, 256)
                    which = (core if side == 0 else 1 - core) * 2 + h
                    old = base[:, which, :, pl.ds(column, 256)].astype(jnp.float32)
                    out[:, which, :, pl.ds(column, 256)] = (old + 0.125 * delta).astype(HALF)

    for step in range(4):
        pl.when(ky == step)(lambda step=step: one(step))


def per_device(
    grad_a, grad_b, factor_a, factor_b, moment_a, second_a, moment_b, second_b, base_rows
):
    f32 = jnp.float32
    shape = jax.ShapeDtypeStruct
    packed = pl.pallas_call(
        pack_kernel,
        out_shape=shape((8, 176, 128), HALF),
        in_specs=[VMEM] * 2,
        out_specs=VMEM,
    )(grad_a, grad_b)
    got = lax.all_to_all(packed, ("zl", "core"), 0, 0, tiled=True)
    sa, sb = shape((2, 64, 128), f32), shape((2, 48, 64), f32)
    new_a, new_b, new_ma, new_va, new_mb, new_vb, send = pl.pallas_call(
        update_kernel,
        out_shape=(sa, sb, sa, sa, sb, sb, shape((8, 176, 128), HALF)),
        in_specs=[VMEM] * 7,
        out_specs=[VMEM] * 7,
    )(got, factor_a, factor_b, moment_a, second_a, moment_b, second_b)
    line = lax.all_to_all(send, ("zl", "zh"), 0, 0, tiled=True)

    def hop(value, axis, k):
        n = lax.axis_size(axis)
        return lax.ppermute(value, axis, [(i, (i + k) % n) for i in range(n)])

    def spread(value, axis):
        return [value] + [hop(value, axis, k) for k in (1, 2, 3)]

    x, y, core, zh = (lax.axis_index(a) for a in ("x", "y", "core", "zh"))
    one = jnp.stack(spread(line[:, 0:64], "x"))
    two = jnp.stack(spread(line[:, 64:128], "y"))
    b_own = lax.dynamic_index_in_dim(
        line.reshape(4, 2, 176, 128)[:, :, 128:176], zh, axis=1, keepdims=False
    )
    pieces = spread(one, "y") + spread(two, "x")
    pieces = pieces + [hop(p, "core", 1) for p in pieces]
    b_sibling = hop(b_own, "core", 1)
    pieces = [p.reshape(4, 4, 2, 64, 128) for p in pieces]
    place = jnp.stack([x, y, core]).astype(jnp.int32)
    block = pl.BlockSpec(
        (4, 4, 48, 1024), lambda ky, place: (0, 0, 0, lax.rem(place[1] + 4 - ky, 4))
    )
    merged = pl.pallas_call(
        merge_kernel,
        out_shape=shape((4, 4, 48, 4096), HALF),
        grid_spec=pltpu.PrefetchScalarGridSpec(
            num_scalar_prefetch=1,
            grid=(4,),
            in_specs=[VMEM, VMEM, block] + [VMEM] * 16,
            out_specs=block,
            scratch_shapes=[pltpu.VMEM((2, 2, 192, 256), HALF)],
        ),
        compiler_params=pltpu.CompilerParams(vmem_limit_bytes=40 * 1024 * 1024),
    )(place, b_own, b_sibling, base_rows.reshape(4, 4, 48, 4096), *pieces)
    return (new_a, new_b, new_ma, new_va, new_mb, new_vb, merged.reshape(16, 48, 4096))


def solution(mesh):
    fine = Mesh(mesh.devices.reshape(4, 2, 4, 4, 2), ("zl", "core", "y", "x", "zh"))
    group, tensor = ("zl", "core"), ("y", "x", "zh")
    in_specs = (
        P(group, None, None, tensor),
        P(group, None, tensor, None),
        P(group, None, tensor),
        P(group, tensor, None),
        P(group, None, tensor),
        P(group, None, tensor),
        P(group, tensor, None),
        P(group, tensor, None),
        P(None, tensor, None),
    )
    out_specs = (
        P(group, None, tensor),
        P(group, tensor, None),
        P(group, None, tensor),
        P(group, None, tensor),
        P(group, tensor, None),
        P(group, tensor, None),
        P(None, tensor, None),
    )
    return jax.shard_map(
        per_device, mesh=fine, in_specs=in_specs, out_specs=out_specs, check_vma=False
    )
```

```python
import functools

import jax
import jax.numpy as jnp
from jax import lax
from jax.experimental import pallas as pl
from jax.experimental.pallas import tpu as pltpu
from jax.sharding import Mesh, PartitionSpec as P

STEP = 100
HALF = jnp.bfloat16
VMEM = pl.BlockSpec(memory_space=pltpu.VMEM)
SMEM = pl.BlockSpec(memory_space=pltpu.SMEM)
HBM = pl.BlockSpec(memory_space=pltpu.HBM)


def cost(size):
    return pl.CostEstimate(flops=0, bytes_accessed=size, transcendentals=0)


def inside(value):
    return pltpu.with_memory_space_constraint(value, pltpu.VMEM)


def adam_update(param, grad, first, second):
    new_first = 0.9 * first + 0.1 * grad
    new_second = 0.999 * second + 0.001 * grad * grad
    corr_first = new_first / (1.0 - 0.9**STEP)
    corr_second = new_second / (1.0 - 0.999**STEP)
    new_param = param - 0.1 * corr_first / (jnp.sqrt(corr_second) + 1e-08)
    return (new_param, new_first, new_second)


def pack_kernel(grad_a, grad_b, out):
    out[:, 0:128, :] = grad_a[0].reshape(8, 128, 128).astype(HALF)
    for owner in range(8):
        pair = jnp.concatenate([grad_b[0, 2 * owner], grad_b[0, 2 * owner + 1]], axis=-1)
        out[owner, 128:176, :] = pair.astype(HALF)


def summed(got):
    total = got[0].astype(jnp.float32)
    for learner in range(1, 8):
        total = total + got[learner].astype(jnp.float32)
    return total


def apart(total):
    return total[0:128].reshape(2, 64, 128), [total[128:176, 64 * e : 64 * e + 64] for e in range(2)]


def send_kernel(got, factor_a, factor_b, moment_a, second_a, moment_b, second_b, send, total):
    total[...] = summed(got)
    grad_a, grad_b = apart(total)
    a = adam_update(factor_a[...], grad_a, moment_a[...], second_a[...])[0]
    b = [adam_update(factor_b[e], grad_b[e], moment_b[e], second_b[e])[0] for e in range(2)]
    a_half = a.astype(HALF).reshape(128, 128)
    b_half = jnp.concatenate(b, axis=-1).astype(HALF)
    for peer in range(8):
        send[peer, 0:128, :] = a_half
        send[peer, 128:176, :] = b_half


def state_kernel(
    total, factor_a, factor_b, moment_a, second_a, moment_b, second_b,
    new_a, new_b, new_ma, new_va, new_mb, new_vb,
):
    grad_a, grad_b = apart(total)
    new_a[...], new_ma[...], new_va[...] = adam_update(
        factor_a[...], grad_a, moment_a[...], second_a[...]
    )
    for e in range(2):
        new_b[e], new_mb[e], new_vb[e] = adam_update(
            factor_b[e], grad_b[e], moment_b[e], second_b[e]
        )


def split_kernel(place, line, half_0, half_1, rows):
    half_0[...] = line[:, 0:64].reshape(512, 128)
    half_1[...] = line[:, 64:128].reshape(512, 128)
    zh = place[0]
    for zl in range(4):
        rows[zl] = line[2 * zl + zh, 128:176]


def join_kernel(*refs):
    rows, mine_0, mine_1, everything = refs[8:]
    for h, mine in ((0, mine_0), (1, mine_1)):
        for k in range(4):
            value = refs[4 * h + k][...]
            mine[512 * k : 512 * k + 512] = value
            everything[2048 * h + 512 * k : 2048 * h + 512 * k + 512] = value
    everything[4096:4288] = rows[...].reshape(192, 128)


def blocks_kernel(rows_own, other, blocks):
    rows_sibling = other[4096:4288].reshape(4, 48, 128)
    for side, rows in ((0, rows_own[...]), (1, rows_sibling)):
        for h in range(2):
            for zl in range(4):
                parts = []
                if zl:
                    parts.append(jnp.zeros((48, 64 * zl), HALF))
                parts.append(rows[zl, :, 64 * h : 64 * h + 64])
                if zl < 3:
                    parts.append(jnp.zeros((48, 192 - 64 * zl), HALF))
                blocks[side, h, 48 * zl : 48 * zl + 48, :] = jnp.concatenate(parts, axis=-1)


def relay_kernel(up_0, up_1, down_0, down_1, half_0, half_1, half_2, half_3, everything):
    half_0[...] = up_0[0:1024]
    half_1[...] = up_1[0:1024]
    half_2[...] = down_0[1024:2048]
    half_3[...] = down_1[1024:2048]
    for k, piece in enumerate((up_0, up_1, down_0, down_1)):
        everything[2048 * k : 2048 * k + 2048] = piece[...]


def merge_kernel(place, blocks, *refs, distances, pick):
    n = len(distances)
    pieces = pick(refs)
    base, out, held, read, write = refs[-5:]
    x, y, core = place[0], place[1], place[2]

    def unit(h, d, inner):
        ky, kx = (distances[d], inner) if h == 0 else (inner, distances[d])
        column = lax.rem(y + 4 - ky, 4) * 1024 + lax.rem(x + 4 - kx, 4) * 256
        return pl.ds(pl.multiple_of(column, 256), 256), (h * n + d) * 4 + inner

    def copy_in(h, d, inner):
        where, u = unit(h, d, inner)
        return pltpu.make_async_copy(base.at[:, :, h, :, where], held.at[u], read.at[u])

    def copy_out(h, d, inner):
        where, u = unit(h, d, inner)
        return pltpu.make_async_copy(held.at[u], out.at[:, :, h, :, where], write.at[u])

    units = [(h, d, inner) for d in range(n) for h in range(2) for inner in range(4)]
    for t in units:
        copy_in(*t).start()
    for d in range(n):
        for h in range(2):
            for inner in range(4):
                copy_in(h, d, inner).wait()
            for side in range(2):
                piece = jnp.concatenate([p[...] for p in pieces[side][h]]).reshape(4, 4, 2, 64, 128)
                wide = jnp.concatenate(
                    [piece[i, :, zh].reshape(256, 128) for i in range(4) for zh in range(2)], axis=-1
                )
                delta = jnp.dot(blocks[side, h], wide, preferred_element_type=jnp.float32)
                owner = core if side == 0 else 1 - core
                for inner in range(4):
                    u = (h * n + d) * 4 + inner
                    old = held[u, :, owner].astype(jnp.float32)
                    part = delta[:, 256 * inner : 256 * inner + 256].reshape(4, 48, 256)
                    held[u, :, owner] = (old + 0.125 * part).astype(HALF)
            for inner in range(4):
                copy_out(h, d, inner).start()
    for t in units:
        copy_out(*t).wait()


def next_merge_kernel(place, blocks, *refs, distances, pick):
    merge_kernel(place, blocks, *refs[:-5], *refs[-4:], distances=distances, pick=pick)


def pick_first(refs):
    return [[[refs[side].at[2048 * h : 2048 * h + 2048]] for h in range(2)] for side in range(2)]


def pick_near(refs, start):
    other = [[refs[2].at[start + 2048 * h : start + 2048 * h + 2048]] for h in range(2)]
    return [[[refs[0]], [refs[1]]], other]


def pick_far(refs):
    return [[[refs[4 * side + h], refs[4 * side + 2 + h]] for h in range(2)] for side in range(2)]


def hop(value, axis, k):
    n = lax.axis_size(axis)
    return lax.ppermute(value, axis, [(i, (i + k) % n) for i in range(n)])


def swap(value, axis, mask):
    n = lax.axis_size(axis)
    return lax.ppermute(value, axis, [(i, i ^ mask) for i in range(n)])


def per_device(
    grad_a, grad_b, factor_a, factor_b, moment_a, second_a, moment_b, second_b, base_rows
):
    f32 = jnp.float32
    shape = jax.ShapeDtypeStruct
    packed = pl.pallas_call(
        pack_kernel,
        out_shape=pltpu.VMEM((8, 176, 128), HALF),
        in_specs=[VMEM] * 2,
        out_specs=VMEM,
    )(grad_a, grad_b)
    got = lax.all_to_all(packed, ("zl", "core"), 0, 0, tiled=True)
    sa, sb = shape((2, 64, 128), f32), shape((2, 48, 64), f32)
    state = (factor_a, factor_b, moment_a, second_a, moment_b, second_b)
    send, total = pl.pallas_call(
        send_kernel,
        out_shape=(pltpu.VMEM((8, 176, 128), HALF), shape((176, 128), f32)),
        in_specs=[VMEM] * 7,
        out_specs=(VMEM,) * 2,
    )(inside(got), *state)
    line = lax.all_to_all(send, ("zl", "zh"), 0, 0, tiled=True)

    x, y, core, zh = (lax.axis_index(a).astype(jnp.int32) for a in ("x", "y", "core", "zh"))
    half_0, half_1, rows_own = pl.pallas_call(
        split_kernel,
        out_shape=(pltpu.VMEM((512, 128), HALF), pltpu.VMEM((512, 128), HALF), pltpu.VMEM((4, 48, 128), HALF)),
        in_specs=[SMEM, VMEM],
        out_specs=(VMEM,) * 3,
    )(zh.reshape(1), inside(line))
    halves = half_0, half_1

    first, second = ("x", "y"), ("y", "x")
    parts = [[halves[h]] + [hop(halves[h], first[h], k) for k in (1, 2, 3)] for h in range(2)]
    parts = lax.optimization_barrier(parts)
    mine_0, mine_1, everything = pl.pallas_call(
        join_kernel,
        out_shape=(shape((2048, 128), HALF),) * 2 + (shape((4288, 128), HALF),),
        in_specs=[VMEM] * 9,
        out_specs=(VMEM,) * 3,
    )(*[inside(p) for p in parts[0] + parts[1]], inside(rows_own))
    mine = mine_0, mine_1
    near = [hop(mine[h], second[h], k) for k in (1, 3) for h in range(2)]
    other = hop(everything, "core", 1)
    blocks = pl.pallas_call(
        blocks_kernel,
        out_shape=pltpu.VMEM((2, 2, 192, 256), HALF),
        in_specs=[VMEM] * 2,
        out_specs=VMEM,
    )(inside(rows_own), inside(other))
    states = pl.pallas_call(
        state_kernel,
        out_shape=(sa, sb, sa, sa, sb, sb),
        in_specs=[VMEM] * 7,
        out_specs=[VMEM] * 6,
        cost_estimate=cost(1024),
    )(total, *state)

    place = jnp.stack([x, y, core])
    base = pltpu.with_memory_space_constraint(base_rows.reshape(4, 2, 2, 48, 4096), pltpu.HBM)

    def merge(distances, pick, pieces, before):
        n = len(distances)
        before = [] if before is None else [before]
        return pl.pallas_call(
            functools.partial(next_merge_kernel if before else merge_kernel, distances=distances, pick=pick),
            out_shape=shape((4, 2, 2, 48, 4096), HALF),
            in_specs=[SMEM, VMEM] + [VMEM] * len(pieces) + [HBM] + [HBM] * len(before),
            out_specs=HBM,
            input_output_aliases={3 + len(pieces): 0} if before else {},
            scratch_shapes=[
                pltpu.VMEM((8 * n, 4, 2, 48, 256), HALF),
                pltpu.SemaphoreType.DMA((8 * n,)),
                pltpu.SemaphoreType.DMA((8 * n,)),
            ],
            compiler_params=pltpu.CompilerParams(vmem_limit_bytes=(6 + 4 * n) * 1024 * 1024),
            cost_estimate=cost(1024),
        )(place, inside(blocks), *pieces, base, *before)

    merged = merge((0,), pick_first, [everything, other], None)
    near, merged, states = lax.optimization_barrier((near, merged, states))
    half = shape((1024, 128), HALF)
    *relayed, everything = pl.pallas_call(
        relay_kernel,
        out_shape=(half,) * 4 + (shape((8192, 128), HALF),),
        in_specs=[VMEM] * 4,
        out_specs=(VMEM,) * 5,
    )(*near)
    far = [hop(relayed[2 * s + h], second[h], 1 + 2 * s) for s in range(2) for h in range(2)]
    near_other = hop(everything, "core", 1)
    merged = merge((1,), functools.partial(pick_near, start=0), near[:2] + [near_other], merged)
    far, merged = lax.optimization_barrier((far, merged))
    far_other = [hop(v, "core", 1) for v in far]
    merged = merge((3,), functools.partial(pick_near, start=4096), near[2:] + [near_other], merged)
    merged = merge((2,), pick_far, far + far_other, merged)
    new_a, new_b, new_ma, new_va, new_mb, new_vb = states
    return (new_a, new_b, new_ma, new_va, new_mb, new_vb, merged.reshape(16, 48, 4096))


def solution(mesh):
    fine = Mesh(mesh.devices.reshape(4, 2, 4, 4, 2), ("zl", "core", "y", "x", "zh"))
    group, tensor = ("zl", "core"), ("y", "x", "zh")
    in_specs = (
        P(group, None, None, tensor),
        P(group, None, tensor, None),
        P(group, None, tensor),
        P(group, tensor, None),
        P(group, None, tensor),
        P(group, None, tensor),
        P(group, tensor, None),
        P(group, tensor, None),
        P(None, tensor, None),
    )
    out_specs = (
        P(group, None, tensor),
        P(group, tensor, None),
        P(group, None, tensor),
        P(group, None, tensor),
        P(group, tensor, None),
        P(group, tensor, None),
        P(None, tensor, None),
    )
    return jax.shard_map(
        per_device, mesh=fine, in_specs=in_specs, out_specs=out_specs, check_vma=False
    )
```

```python
import functools

import jax
import jax.numpy as jnp
from jax import lax
from jax.experimental import pallas as pl
from jax.experimental.pallas import tpu as pltpu
from jax.sharding import Mesh, PartitionSpec as P

STEP = 100
HALF = jnp.bfloat16
VMEM = pl.BlockSpec(memory_space=pltpu.VMEM)
SMEM = pl.BlockSpec(memory_space=pltpu.SMEM)
HBM = pl.BlockSpec(memory_space=pltpu.HBM)


def cost(size):
    return pl.CostEstimate(flops=0, bytes_accessed=size, transcendentals=0)


def limit(size):
    return pltpu.CompilerParams(vmem_limit_bytes=size * 2**20)


def inside(value):
    return pltpu.with_memory_space_constraint(value, pltpu.VMEM)


def adam_update(param, grad, first, second):
    new_first = 0.9 * first + 0.1 * grad
    new_second = 0.999 * second + 0.001 * grad * grad
    corr_first = new_first / (1.0 - 0.9**STEP)
    corr_second = new_second / (1.0 - 0.999**STEP)
    new_param = param - 0.1 * corr_first / (jnp.sqrt(corr_second) + 1e-08)
    return (new_param, new_first, new_second)


def fetched(there, here, sems):
    copies = [pltpu.make_async_copy(t, h, sems.at[i]) for i, (t, h) in enumerate(zip(there, here))]
    for copy in copies:
        copy.start()
    return copies


def pack_kernel(*refs):
    there, out, here = refs[:8], refs[8], refs[9:15]
    grad_a, grad_b, sems = refs[15:]
    copies = fetched(there, (grad_a, grad_b, *here), sems)
    copies[0].wait()
    copies[1].wait()
    out[:, 0:128, :] = grad_a[0].reshape(8, 128, 128).astype(HALF)
    for owner in range(8):
        pair = jnp.concatenate([grad_b[0, 2 * owner], grad_b[0, 2 * owner + 1]], axis=-1)
        out[owner, 128:176, :] = pair.astype(HALF)
    for copy in copies[2:]:
        copy.wait()


def summed(got):
    total = got[0].astype(jnp.float32)
    for learner in range(1, 8):
        total = total + got[learner].astype(jnp.float32)
    return total


def apart(total):
    return total[0:128].reshape(2, 64, 128), [total[128:176, 64 * e : 64 * e + 64] for e in range(2)]


def send_kernel(got, factor_a, factor_b, moment_a, second_a, moment_b, second_b, send, total):
    total[...] = summed(got)
    grad_a, grad_b = apart(total)
    a = adam_update(factor_a[...], grad_a, moment_a[...], second_a[...])[0]
    b = [adam_update(factor_b[e], grad_b[e], moment_b[e], second_b[e])[0] for e in range(2)]
    a_half = a.astype(HALF).reshape(128, 128)
    b_half = jnp.concatenate(b, axis=-1).astype(HALF)
    for peer in range(8):
        send[peer, 0:128, :] = a_half
        send[peer, 128:176, :] = b_half


def state_kernel(
    total, factor_a, factor_b, moment_a, second_a, moment_b, second_b,
    new_a, new_b, new_ma, new_va, new_mb, new_vb,
):
    grad_a, grad_b = apart(total)
    new_a[...], new_ma[...], new_va[...] = adam_update(
        factor_a[...], grad_a, moment_a[...], second_a[...]
    )
    for e in range(2):
        new_b[e], new_mb[e], new_vb[e] = adam_update(
            factor_b[e], grad_b[e], moment_b[e], second_b[e]
        )


def split_kernel(place, line, half_0, half_1, rows):
    half_0[...] = line[:, 0:64].reshape(512, 128)
    half_1[...] = line[:, 64:128].reshape(512, 128)
    zh = place[0]
    for zl in range(4):
        rows[zl] = line[2 * zl + zh, 128:176]


def join_kernel(*refs):
    rows, mine_0, mine_1, everything = refs[8:]
    for h, mine in ((0, mine_0), (1, mine_1)):
        for k in range(4):
            value = refs[4 * h + k][...]
            mine[512 * k : 512 * k + 512] = value
            everything[2048 * h + 512 * k : 2048 * h + 512 * k + 512] = value
    everything[4096:4288] = rows[...].reshape(192, 128)


def blocks_kernel(rows_own, other, blocks):
    rows_sibling = other[4096:4288].reshape(4, 48, 128)
    for side, rows in ((0, rows_own[...]), (1, rows_sibling)):
        for h in range(2):
            for zl in range(4):
                parts = []
                if zl:
                    parts.append(jnp.zeros((48, 64 * zl), HALF))
                parts.append(rows[zl, :, 64 * h : 64 * h + 64])
                if zl < 3:
                    parts.append(jnp.zeros((48, 192 - 64 * zl), HALF))
                blocks[side, h, 48 * zl : 48 * zl + 48, :] = jnp.concatenate(parts, axis=-1)


def relay_kernel(up_0, up_1, down_0, down_1, half_0, half_1, half_2, half_3, everything):
    half_0[...] = up_0[0:1024]
    half_1[...] = up_1[0:1024]
    half_2[...] = down_0[1024:2048]
    half_3[...] = down_1[1024:2048]
    for k, piece in enumerate((up_0, up_1, down_0, down_1)):
        everything[2048 * k : 2048 * k + 2048] = piece[...]


def stash_kernel(base, kept, sems):
    for copy in fetched([base.at[zl] for zl in range(4)], [kept.at[zl] for zl in range(4)], sems):
        copy.wait()


def merge_kernel(place, blocks, base, *refs, distances, pick):
    n = len(distances)
    out, held, write = refs[-3:]
    x, y, core = place[0], place[1], place[2]

    def unit(d, h, inner):
        ky, kx = (distances[d], inner) if h == 0 else (inner, distances[d])
        column = lax.rem(y + 4 - ky, 4) * 1024 + lax.rem(x + 4 - kx, 4) * 256
        return pl.ds(pl.multiple_of(column, 256), 256), (d * 2 + h) * 4 + inner

    def copy_out(d, h, inner):
        where, u = unit(d, h, inner)
        return pltpu.make_async_copy(held.at[u], out.at[:, :, h, :, where], write.at[u])

    units = [(d, h, inner) for d in range(n) for h in range(2) for inner in range(4)]
    for d, h, inner in units:
        where, u = unit(d, h, inner)
        for side in range(2):
            ref, row = pick(refs, side, d, h, inner)
            piece = ref[row : row + 512].reshape(4, 2, 64, 128)
            wide = jnp.concatenate([piece[:, zh].reshape(256, 128) for zh in range(2)], axis=-1)
            delta = jnp.dot(blocks[side, h], wide, preferred_element_type=jnp.float32)
            owner = core if side == 0 else 1 - core
            old = base[:, owner, h, :, where].astype(jnp.float32)
            held[u, :, owner] = (old + 0.125 * delta.reshape(4, 48, 256)).astype(HALF)
        copy_out(d, h, inner).start()
    for t in units:
        copy_out(*t).wait()


def next_merge_kernel(place, blocks, base, *refs, **how):
    merge_kernel(place, blocks, base, *refs[:-4], *refs[-3:], **how)


def pick_first(refs, side, d, h, inner):
    return refs[side], 2048 * h + 512 * inner


def pick_near(refs, side, d, h, inner):
    if side == 0:
        return refs[2 * d + h], 512 * inner
    return refs[4], 2048 * (2 * d + h) + 512 * inner


def pick_far(refs, side, d, h, inner):
    return refs[4 * side + 2 * (inner // 2) + h], 512 * (inner % 2)


def hop(value, axis, k):
    n = lax.axis_size(axis)
    return lax.ppermute(value, axis, [(i, (i + k) % n) for i in range(n)])


def swap(value, axis, mask):
    n = lax.axis_size(axis)
    return lax.ppermute(value, axis, [(i, i ^ mask) for i in range(n)])


def per_device(
    grad_a, grad_b, factor_a, factor_b, moment_a, second_a, moment_b, second_b, base_rows
):
    f32 = jnp.float32
    shape = jax.ShapeDtypeStruct
    sa, sb = shape((2, 64, 128), f32), shape((2, 48, 64), f32)
    needed = (grad_a, grad_b, factor_a, factor_b, moment_a, second_a, moment_b, second_b)
    packed, *state = pl.pallas_call(
        pack_kernel,
        out_shape=[pltpu.VMEM((8, 176, 128), HALF)] + [pltpu.VMEM(v.shape, f32) for v in needed[2:]],
        in_specs=[HBM] * 8,
        out_specs=[VMEM] * 7,
        scratch_shapes=[pltpu.VMEM(v.shape, f32) for v in needed[:2]] + [pltpu.SemaphoreType.DMA((8,))],
        compiler_params=limit(4),
    )(*[pltpu.with_memory_space_constraint(v, pltpu.HBM) for v in needed])
    got = lax.all_to_all(packed, ("zl", "core"), 0, 0, tiled=True)
    state = [inside(v) for v in state]
    send, total = pl.pallas_call(
        send_kernel,
        out_shape=(pltpu.VMEM((8, 176, 128), HALF), pltpu.VMEM((176, 128), f32)),
        in_specs=[VMEM] * 7,
        out_specs=(VMEM,) * 2,
        compiler_params=limit(4),
    )(inside(got), *state)
    line = lax.all_to_all(send, ("zl", "zh"), 0, 0, tiled=True)

    x, y, core, zh = (lax.axis_index(a).astype(jnp.int32) for a in ("x", "y", "core", "zh"))
    half_0, half_1, rows_own = pl.pallas_call(
        split_kernel,
        out_shape=(pltpu.VMEM((512, 128), HALF), pltpu.VMEM((512, 128), HALF), pltpu.VMEM((4, 48, 128), HALF)),
        in_specs=[SMEM, VMEM],
        out_specs=(VMEM,) * 3,
        compiler_params=limit(4),
    )(zh.reshape(1), inside(line))
    halves = half_0, half_1

    first, second = ("x", "y"), ("y", "x")
    parts = [[halves[h]] + [hop(halves[h], first[h], k) for k in (1, 2, 3)] for h in range(2)]
    parts = lax.optimization_barrier(parts)
    mine_0, mine_1, everything = pl.pallas_call(
        join_kernel,
        out_shape=(pltpu.VMEM((2048, 128), HALF),) * 2 + (pltpu.VMEM((4288, 128), HALF),),
        in_specs=[VMEM] * 9,
        out_specs=(VMEM,) * 3,
        compiler_params=limit(6),
    )(*[inside(p) for p in parts[0] + parts[1]], inside(rows_own))
    mine = mine_0, mine_1
    near = [hop(mine[h], second[h], k) for k in (1, 3) for h in range(2)]
    other = hop(everything, "core", 1)
    base, mine_0 = lax.optimization_barrier((base_rows, mine_0))
    base = pl.pallas_call(
        stash_kernel,
        out_shape=pltpu.VMEM((4, 2, 2, 48, 4096), HALF),
        in_specs=[HBM],
        out_specs=VMEM,
        scratch_shapes=[pltpu.SemaphoreType.DMA((4,))],
        compiler_params=limit(2),
        cost_estimate=cost(1024),
    )(pltpu.with_memory_space_constraint(base.reshape(4, 2, 2, 48, 4096), pltpu.HBM))
    blocks = pl.pallas_call(
        blocks_kernel,
        out_shape=pltpu.VMEM((2, 2, 192, 256), HALF),
        in_specs=[VMEM] * 2,
        out_specs=VMEM,
        compiler_params=limit(4),
    )(inside(rows_own), inside(other))
    states = pl.pallas_call(
        state_kernel,
        out_shape=(sa, sb, sa, sa, sb, sb),
        in_specs=[VMEM] * 7,
        out_specs=[VMEM] * 6,
        compiler_params=limit(4),
        cost_estimate=cost(1024),
    )(inside(total), *state)

    place = jnp.stack([x, y, core])

    def merge(distances, pick, pieces, before):
        n = len(distances)
        before = [] if before is None else [before]
        return pl.pallas_call(
            functools.partial(next_merge_kernel if before else merge_kernel, distances=distances, pick=pick),
            out_shape=shape((4, 2, 2, 48, 4096), HALF),
            in_specs=[SMEM, VMEM, VMEM] + [VMEM] * len(pieces) + [HBM] * len(before),
            out_specs=HBM,
            input_output_aliases={3 + len(pieces): 0} if before else {},
            scratch_shapes=[
                pltpu.VMEM((8 * n, 4, 2, 48, 256), HALF),
                pltpu.SemaphoreType.DMA((8 * n,)),
            ],
            compiler_params=limit(2 + 2 * n),
            cost_estimate=cost(1024),
        )(place, inside(blocks), inside(base), *[inside(v) for v in pieces], *before)

    merged = merge((0,), pick_first, [everything, other], None)
    near, merged, states = lax.optimization_barrier((near, merged, states))
    half = shape((1024, 128), HALF)
    *relayed, everything = pl.pallas_call(
        relay_kernel,
        out_shape=(half,) * 4 + (shape((8192, 128), HALF),),
        in_specs=[VMEM] * 4,
        out_specs=(VMEM,) * 5,
        compiler_params=limit(8),
    )(*near)
    far = [hop(relayed[2 * s + h], second[h], 1 + 2 * s) for s in range(2) for h in range(2)]
    near_other = hop(everything, "core", 1)
    merged = merge((1, 3), pick_near, [*near, near_other], merged)
    far, merged = lax.optimization_barrier((far, merged))
    far_other = [hop(v, "core", 1) for v in far]
    merged = merge((2,), pick_far, far + far_other, merged)
    new_a, new_b, new_ma, new_va, new_mb, new_vb = states
    return (new_a, new_b, new_ma, new_va, new_mb, new_vb, merged.reshape(16, 48, 4096))


def solution(mesh):
    fine = Mesh(mesh.devices.reshape(4, 2, 4, 4, 2), ("zl", "core", "y", "x", "zh"))
    group, tensor = ("zl", "core"), ("y", "x", "zh")
    in_specs = (
        P(group, None, None, tensor),
        P(group, None, tensor, None),
        P(group, None, tensor),
        P(group, tensor, None),
        P(group, None, tensor),
        P(group, None, tensor),
        P(group, tensor, None),
        P(group, tensor, None),
        P(None, tensor, None),
    )
    out_specs = (
        P(group, None, tensor),
        P(group, tensor, None),
        P(group, None, tensor),
        P(group, None, tensor),
        P(group, tensor, None),
        P(group, tensor, None),
        P(None, tensor, None),
    )
    return jax.shard_map(
        per_device, mesh=fine, in_specs=in_specs, out_specs=out_specs, check_vma=False
    )
```

```python
import functools

import jax
import jax.numpy as jnp
from jax import lax
from jax.experimental import pallas as pl
from jax.experimental.pallas import tpu as pltpu
from jax.sharding import Mesh, PartitionSpec as P

STEP = 100
HALF = jnp.bfloat16
VMEM = pl.BlockSpec(memory_space=pltpu.VMEM)
SMEM = pl.BlockSpec(memory_space=pltpu.SMEM)
HBM = pl.BlockSpec(memory_space=pltpu.HBM)


def cost(size):
    return pl.CostEstimate(flops=0, bytes_accessed=size, transcendentals=0)


def limit(size):
    return pltpu.CompilerParams(vmem_limit_bytes=size * 2**20)


def inside(value):
    return pltpu.with_memory_space_constraint(value, pltpu.VMEM)


def adam_update(param, grad, first, second):
    new_first = 0.9 * first + 0.1 * grad
    new_second = 0.999 * second + 0.001 * grad * grad
    corr_first = new_first / (1.0 - 0.9**STEP)
    corr_second = new_second / (1.0 - 0.999**STEP)
    new_param = param - 0.1 * corr_first / (jnp.sqrt(corr_second) + 1e-08)
    return (new_param, new_first, new_second)


def fetched(there, here, sems):
    copies = [pltpu.make_async_copy(t, h, sems.at[i]) for i, (t, h) in enumerate(zip(there, here))]
    for copy in copies:
        copy.start()
    return copies


def pack_kernel(*refs):
    there, out, here = refs[:8], refs[8], refs[9:15]
    grad_a, grad_b, sems = refs[15:]
    copies = fetched(there, (grad_a, grad_b, *here), sems)
    copies[0].wait()
    copies[1].wait()
    out[:, 0:128, :] = grad_a[0].reshape(8, 128, 128).astype(HALF)
    for owner in range(8):
        pair = jnp.concatenate([grad_b[0, 2 * owner], grad_b[0, 2 * owner + 1]], axis=-1)
        out[owner, 128:176, :] = pair.astype(HALF)
    for copy in copies[2:]:
        copy.wait()


def summed(got):
    total = got[0].astype(jnp.float32)
    for learner in range(1, 8):
        total = total + got[learner].astype(jnp.float32)
    return total


def apart(total):
    return total[0:128].reshape(2, 64, 128), [total[128:176, 64 * e : 64 * e + 64] for e in range(2)]


def send_kernel(got, factor_a, factor_b, moment_a, second_a, moment_b, second_b, send, total):
    total[...] = summed(got)
    grad_a, grad_b = apart(total)
    a = adam_update(factor_a[...], grad_a, moment_a[...], second_a[...])[0]
    b = [adam_update(factor_b[e], grad_b[e], moment_b[e], second_b[e])[0] for e in range(2)]
    a_half = a.astype(HALF).reshape(128, 128)
    b_half = jnp.concatenate(b, axis=-1).astype(HALF)
    for peer in range(8):
        send[peer, 0:128, :] = a_half
        send[peer, 128:176, :] = b_half


def state_kernel(total, *refs):
    there, (new_a, new_b, new_ma, new_va, new_mb, new_vb) = refs[:6], refs[6:12]
    here, sems = refs[12:18], refs[18]
    for copy in fetched(there, here, sems):
        copy.wait()
    factor_a, factor_b, moment_a, second_a, moment_b, second_b = here
    grad_a, grad_b = apart(total)
    new_a[...], new_ma[...], new_va[...] = adam_update(
        factor_a[...], grad_a, moment_a[...], second_a[...]
    )
    for e in range(2):
        new_b[e], new_mb[e], new_vb[e] = adam_update(
            factor_b[e], grad_b[e], moment_b[e], second_b[e]
        )


def split_kernel(place, line, half_0, half_1, rows):
    half_0[...] = line[:, 0:64].reshape(512, 128)
    half_1[...] = line[:, 64:128].reshape(512, 128)
    zh = place[0]
    for zl in range(4):
        rows[zl] = line[2 * zl + zh, 128:176]


def join_kernel(*refs):
    rows, mine_0, mine_1, everything = refs[8:]
    for h, mine in ((0, mine_0), (1, mine_1)):
        for k in range(4):
            value = refs[4 * h + k][...]
            mine[512 * k : 512 * k + 512] = value
            everything[2048 * h + 512 * k : 2048 * h + 512 * k + 512] = value
    everything[4096:4288] = rows[...].reshape(192, 128)


def blocks_kernel(rows_own, other, blocks):
    rows_sibling = other[4096:4288].reshape(4, 48, 128)
    for side, rows in ((0, rows_own[...]), (1, rows_sibling)):
        for h in range(2):
            for zl in range(4):
                parts = []
                if zl:
                    parts.append(jnp.zeros((48, 64 * zl), HALF))
                parts.append(rows[zl, :, 64 * h : 64 * h + 64])
                if zl < 3:
                    parts.append(jnp.zeros((48, 192 - 64 * zl), HALF))
                blocks[side, h, 48 * zl : 48 * zl + 48, :] = jnp.concatenate(parts, axis=-1)


def relay_kernel(up_0, up_1, down_0, down_1, half_0, half_1, half_2, half_3, everything):
    half_0[...] = up_0[0:1024]
    half_1[...] = up_1[0:1024]
    half_2[...] = down_0[1024:2048]
    half_3[...] = down_1[1024:2048]
    for k, piece in enumerate((up_0, up_1, down_0, down_1)):
        everything[2048 * k : 2048 * k + 2048] = piece[...]


def stash_kernel(base, kept, sems):
    for copy in fetched([base.at[zl] for zl in range(4)], [kept.at[zl] for zl in range(4)], sems):
        copy.wait()


def merge_kernel(place, blocks, base, *refs, distances, pick):
    out, held_0, held_1, write = refs[-4:]
    x, y, core = place[0], place[1], place[2]

    def column(kx, ky):
        return (x ^ kx) * 256, (y ^ ky) * 1024

    def copy_0(d):
        rows = column(0, distances[d])[1]
        return pltpu.make_async_copy(
            held_0.at[d], out.at[:, :, 0, :, pl.ds(pl.multiple_of(rows, 1024), 1024)], write.at[5 * d]
        )

    def copy_1(d, inner):
        where = pl.multiple_of(sum(column(distances[d], inner)), 256)
        return pltpu.make_async_copy(
            held_1.at[d, inner], out.at[:, :, 1, :, pl.ds(where, 256)], write.at[5 * d + 1 + inner]
        )

    copies = []
    for d, distance in enumerate(distances):
        for h in range(2):
            for inner in range(4):
                kx, ky = (inner, distance) if h == 0 else (distance, inner)
                near, far = column(kx, ky)
                where = pl.ds(pl.multiple_of(near + far, 256), 256)
                for side in range(2):
                    ref, row = pick(refs, side, d, h, inner)
                    piece = ref[row : row + 512].reshape(4, 2, 64, 128)
                    wide = jnp.concatenate([piece[:, zh].reshape(256, 128) for zh in range(2)], axis=-1)
                    delta = jnp.dot(blocks[side, h], wide, preferred_element_type=jnp.float32)
                    owner = core if side == 0 else 1 - core
                    old = base[:, owner, h, :, where].astype(jnp.float32)
                    new = (old + 0.125 * delta.reshape(4, 48, 256)).astype(HALF)
                    if h == 0:
                        held_0[d, :, owner, :, pl.ds(pl.multiple_of(near, 256), 256)] = new
                    else:
                        held_1[d, inner, :, owner] = new
                if h == 1:
                    copies.append(copy_1(d, inner))
                    copies[-1].start()
            if h == 0:
                copies.append(copy_0(d))
                copies[-1].start()
    for copy in copies:
        copy.wait()


def next_merge_kernel(place, blocks, base, *refs, **how):
    merge_kernel(place, blocks, base, *refs[:-5], *refs[-4:], **how)


def pick_first(refs, side, d, h, inner):
    return refs[side], 2048 * h + 512 * inner


def pick_near(refs, side, d, h, inner):
    if side == 0:
        return refs[2 * d + h], 512 * inner
    return refs[4], 2048 * (2 * d + h) + 512 * inner


def pick_far(refs, side, d, h, inner):
    return refs[4 * side + 2 * (inner // 2) + h], 512 * (inner % 2)


def hop(value, axis, k):
    n = lax.axis_size(axis)
    return lax.ppermute(value, axis, [(i, i ^ k) for i in range(n)])


def swap(value, axis, mask):
    n = lax.axis_size(axis)
    return lax.ppermute(value, axis, [(i, i ^ mask) for i in range(n)])


def per_device(
    grad_a, grad_b, factor_a, factor_b, moment_a, second_a, moment_b, second_b, base_rows
):
    f32 = jnp.float32
    shape = jax.ShapeDtypeStruct
    sa, sb = shape((2, 64, 128), f32), shape((2, 48, 64), f32)
    needed = (grad_a, grad_b, factor_a, factor_b, moment_a, second_a, moment_b, second_b)
    packed, *state = pl.pallas_call(
        pack_kernel,
        out_shape=[pltpu.VMEM((8, 176, 128), HALF)] + [pltpu.VMEM(v.shape, f32) for v in needed[2:]],
        in_specs=[HBM] * 8,
        out_specs=[VMEM] * 7,
        scratch_shapes=[pltpu.VMEM(v.shape, f32) for v in needed[:2]] + [pltpu.SemaphoreType.DMA((8,))],
        compiler_params=limit(4),
    )(*[pltpu.with_memory_space_constraint(v, pltpu.HBM) for v in needed])
    got = lax.all_to_all(packed, ("zl", "core"), 0, 0, tiled=True)
    state = [inside(v) for v in state]
    send, total = pl.pallas_call(
        send_kernel,
        out_shape=(pltpu.VMEM((8, 176, 128), HALF), pltpu.VMEM((176, 128), f32)),
        in_specs=[VMEM] * 7,
        out_specs=(VMEM,) * 2,
        compiler_params=limit(4),
    )(inside(got), *state)
    line = lax.all_to_all(send, ("zl", "zh"), 0, 0, tiled=True)

    x, y, core, zh = (lax.axis_index(a).astype(jnp.int32) for a in ("x", "y", "core", "zh"))
    half_0, half_1, rows_own = pl.pallas_call(
        split_kernel,
        out_shape=(pltpu.VMEM((512, 128), HALF), pltpu.VMEM((512, 128), HALF), pltpu.VMEM((4, 48, 128), HALF)),
        in_specs=[SMEM, VMEM],
        out_specs=(VMEM,) * 3,
        compiler_params=limit(4),
    )(zh.reshape(1), inside(line))
    halves = half_0, half_1

    first, second = ("x", "y"), ("y", "x")
    parts = [[halves[h]] + [hop(halves[h], first[h], k) for k in (1, 2, 3)] for h in range(2)]
    parts = lax.optimization_barrier(parts)
    mine_0, mine_1, everything = pl.pallas_call(
        join_kernel,
        out_shape=(pltpu.VMEM((2048, 128), HALF),) * 2 + (pltpu.VMEM((4288, 128), HALF),),
        in_specs=[VMEM] * 9,
        out_specs=(VMEM,) * 3,
        compiler_params=limit(6),
    )(*[inside(p) for p in parts[0] + parts[1]], inside(rows_own))
    mine = mine_0, mine_1
    near = [hop(mine[h], second[h], k) for k in (1, 3) for h in range(2)]
    other = hop(everything, "core", 1)
    base, mine_0 = lax.optimization_barrier((base_rows, mine_0))
    base = pl.pallas_call(
        stash_kernel,
        out_shape=pltpu.VMEM((4, 2, 2, 48, 4096), HALF),
        in_specs=[HBM],
        out_specs=VMEM,
        scratch_shapes=[pltpu.SemaphoreType.DMA((4,))],
        compiler_params=limit(2),
        cost_estimate=cost(1024),
    )(pltpu.with_memory_space_constraint(base.reshape(4, 2, 2, 48, 4096), pltpu.HBM))
    blocks = pl.pallas_call(
        blocks_kernel,
        out_shape=pltpu.VMEM((2, 2, 192, 256), HALF),
        in_specs=[VMEM] * 2,
        out_specs=VMEM,
        compiler_params=limit(4),
    )(inside(rows_own), inside(other))
    states = pl.pallas_call(
        state_kernel,
        out_shape=(sa, sb, sa, sa, sb, sb),
        in_specs=[VMEM] + [HBM] * 6,
        out_specs=[VMEM] * 6,
        scratch_shapes=[pltpu.VMEM(v.shape, f32) for v in needed[2:]] + [pltpu.SemaphoreType.DMA((6,))],
        compiler_params=limit(4),
        cost_estimate=cost(1024),
    )(inside(total), *[pltpu.with_memory_space_constraint(v, pltpu.HBM) for v in needed[2:]])

    place = jnp.stack([x, y, core])

    def merge(distances, pick, pieces, before):
        n = len(distances)
        before = [] if before is None else [before]
        return pl.pallas_call(
            functools.partial(next_merge_kernel if before else merge_kernel, distances=distances, pick=pick),
            out_shape=shape((4, 2, 2, 48, 4096), HALF),
            in_specs=[SMEM, VMEM, VMEM] + [VMEM] * len(pieces) + [HBM] * len(before),
            out_specs=HBM,
            input_output_aliases={3 + len(pieces): 0} if before else {},
            scratch_shapes=[
                pltpu.VMEM((n, 4, 2, 48, 1024), HALF),
                pltpu.VMEM((n, 4, 4, 2, 48, 256), HALF),
                pltpu.SemaphoreType.DMA((5 * n,)),
            ],
            compiler_params=limit(2 + 2 * n),
            cost_estimate=cost(1024),
        )(place, inside(blocks), inside(base), *[inside(v) for v in pieces], *before)

    merged = merge((0,), pick_first, [everything, other], None)
    near, merged, states = lax.optimization_barrier((near, merged, states))
    half = shape((1024, 128), HALF)
    *relayed, everything = pl.pallas_call(
        relay_kernel,
        out_shape=(half,) * 4 + (shape((8192, 128), HALF),),
        in_specs=[VMEM] * 4,
        out_specs=(VMEM,) * 5,
        compiler_params=limit(8),
    )(*near)
    far = [hop(relayed[2 * s + h], second[h], 3 - 2 * s) for s in range(2) for h in range(2)]
    near_other = hop(everything, "core", 1)
    merged = merge((1, 3), pick_near, [*near, near_other], merged)
    far, merged = lax.optimization_barrier((far, merged))
    far_other = [hop(v, "core", 1) for v in far]
    merged = merge((2,), pick_far, far + far_other, merged)
    new_a, new_b, new_ma, new_va, new_mb, new_vb = states
    return (new_a, new_b, new_ma, new_va, new_mb, new_vb, merged.reshape(16, 48, 4096))


def solution(mesh):
    fine = Mesh(mesh.devices.reshape(4, 2, 4, 4, 2), ("zl", "core", "y", "x", "zh"))
    group, tensor = ("zl", "core"), ("y", "x", "zh")
    in_specs = (
        P(group, None, None, tensor),
        P(group, None, tensor, None),
        P(group, None, tensor),
        P(group, tensor, None),
        P(group, None, tensor),
        P(group, None, tensor),
        P(group, tensor, None),
        P(group, tensor, None),
        P(None, tensor, None),
    )
    out_specs = (
        P(group, None, tensor),
        P(group, tensor, None),
        P(group, None, tensor),
        P(group, None, tensor),
        P(group, tensor, None),
        P(group, tensor, None),
        P(None, tensor, None),
    )
    return jax.shard_map(
        per_device, mesh=fine, in_specs=in_specs, out_specs=out_specs, check_vma=False
    )
```

```python
import functools

import jax
import jax.numpy as jnp
from jax import lax
from jax.experimental import pallas as pl
from jax.experimental.pallas import tpu as pltpu
from jax.sharding import Mesh, PartitionSpec as P

STEP = 100
HALF = jnp.bfloat16
VMEM = pl.BlockSpec(memory_space=pltpu.VMEM)
SMEM = pl.BlockSpec(memory_space=pltpu.SMEM)
HBM = pl.BlockSpec(memory_space=pltpu.HBM)


def cost(size):
    return pl.CostEstimate(flops=0, bytes_accessed=size, transcendentals=0)


def limit(size):
    return pltpu.CompilerParams(vmem_limit_bytes=size * 2**20)


def inside(value):
    return pltpu.with_memory_space_constraint(value, pltpu.VMEM)


def adam_update(param, grad, first, second):
    new_first = 0.9 * first + 0.1 * grad
    new_second = 0.999 * second + 0.001 * grad * grad
    corr_first = new_first / (1.0 - 0.9**STEP)
    corr_second = new_second / (1.0 - 0.999**STEP)
    new_param = param - 0.1 * corr_first / (jnp.sqrt(corr_second) + 1e-08)
    return (new_param, new_first, new_second)


def fetched(there, here, sems):
    copies = [pltpu.make_async_copy(t, h, sems.at[i]) for i, (t, h) in enumerate(zip(there, here))]
    for copy in copies:
        copy.start()
    return copies


def pack_kernel(place, *refs):
    there, (keep, give), here = refs[:8], refs[8:10], refs[10:16]
    grad_a, grad_b, sems = refs[16:]
    copies = fetched(there, (grad_a, grad_b, *here), sems)
    copies[0].wait()
    copies[1].wait()
    core = place[0]
    for out, owner_core in ((keep, core), (give, 1 - core)):
        for zl in range(4):
            expert = 4 * zl + 2 * owner_core
            out[zl, 0:128] = grad_a[0, pl.ds(expert, 2)].reshape(128, 128).astype(out.dtype)
            both = jnp.concatenate([grad_b[0, expert], grad_b[0, expert + 1]], axis=-1)
            out[zl, 128:176] = both.astype(out.dtype)
    for copy in copies[2:]:
        copy.wait()


def pair_sum_kernel(place, keep, given, own, out_1, out_2, out_3):
    zl = place[1]
    own[...] = keep[zl] + given[zl].astype(jnp.float32)
    for a, out in ((1, out_1), (2, out_2), (3, out_3)):
        out[...] = (keep[zl ^ a] + given[zl ^ a].astype(jnp.float32)).astype(HALF)


def apart(total):
    return total[0:128].reshape(2, 64, 128), [total[128:176, 64 * e : 64 * e + 64] for e in range(2)]


def send_kernel(
    own, got_1, got_2, got_3, factor_a, factor_b, moment_a, second_a, moment_b, second_b, send, send_a, total
):
    total[...] = own[...] + (got_1[...].astype(jnp.float32) + (got_2[...].astype(jnp.float32) + got_3[...].astype(jnp.float32)))
    grad_a, grad_b = apart(total)
    a = adam_update(factor_a[...], grad_a, moment_a[...], second_a[...])[0]
    b = [adam_update(factor_b[e], grad_b[e], moment_b[e], second_b[e])[0] for e in range(2)]
    a_half = a.astype(HALF).reshape(128, 128)
    b_half = jnp.concatenate(b, axis=-1).astype(HALF)
    send[0:128] = a_half
    send[128:176] = b_half
    send_a[...] = a_half


def state_kernel(total, *refs):
    there, (new_a, new_b, new_ma, new_va, new_mb, new_vb) = refs[:6], refs[6:12]
    here, sems = refs[12:18], refs[18]
    for copy in fetched(there, here, sems):
        copy.wait()
    factor_a, factor_b, moment_a, second_a, moment_b, second_b = here
    grad_a, grad_b = apart(total)
    new_a[...], new_ma[...], new_va[...] = adam_update(
        factor_a[...], grad_a, moment_a[...], second_a[...]
    )
    for e in range(2):
        new_b[e], new_mb[e], new_vb[e] = adam_update(
            factor_b[e], grad_b[e], moment_b[e], second_b[e]
        )


def pair_kernel(send, across, pair):
    pair[0:128] = send[0:128]
    pair[128:256] = across[...]
    pair[256:304] = send[128:176]


def split_kernel(place, *refs):
    half_0, half_1, rows = refs[4:]
    zl, zh = place[0], place[1]
    for a in range(4):
        for b in range(2):
            slot = (zl ^ a) * 2 + (zh ^ b)
            half_0[slot] = refs[a][128 * b : 128 * b + 64]
            half_1[slot] = refs[a][128 * b + 64 : 128 * b + 128]
        rows[zl ^ a] = refs[a][256:304]


def join_kernel(*refs):
    rows, mine_0, mine_1, everything = refs[8:]
    for h, mine in ((0, mine_0), (1, mine_1)):
        for k in range(4):
            value = refs[4 * h + k][...]
            mine[512 * k : 512 * k + 512] = value
            everything[2048 * h + 512 * k : 2048 * h + 512 * k + 512] = value
    everything[4096:4288] = rows[...].reshape(192, 128)


def blocks_kernel(rows_own, other, blocks):
    rows_sibling = other[4096:4288].reshape(4, 48, 128)
    for side, rows in ((0, rows_own[...]), (1, rows_sibling)):
        for h in range(2):
            for zl in range(4):
                parts = []
                if zl:
                    parts.append(jnp.zeros((48, 64 * zl), HALF))
                parts.append(rows[zl, :, 64 * h : 64 * h + 64])
                if zl < 3:
                    parts.append(jnp.zeros((48, 192 - 64 * zl), HALF))
                blocks[side, h, 48 * zl : 48 * zl + 48, :] = jnp.concatenate(parts, axis=-1)


def relay_kernel(up_0, up_1, down_0, down_1, half_0, half_1, half_2, half_3, everything):
    half_0[...] = up_0[0:1024]
    half_1[...] = up_1[0:1024]
    half_2[...] = down_0[1024:2048]
    half_3[...] = down_1[1024:2048]
    for k, piece in enumerate((up_0, up_1, down_0, down_1)):
        everything[2048 * k : 2048 * k + 2048] = piece[...]


def stash_kernel(base, kept, sems):
    for copy in fetched([base.at[zl] for zl in range(4)], [kept.at[zl] for zl in range(4)], sems):
        copy.wait()


def merge_kernel(place, blocks, base, *refs, distances, pick):
    out, held_0, held_1, write = refs[-4:]
    x, y, core = place[0], place[1], place[2]

    def column(kx, ky):
        return (x ^ kx) * 256, (y ^ ky) * 1024

    def copy_0(d):
        rows = column(0, distances[d])[1]
        return pltpu.make_async_copy(
            held_0.at[d], out.at[:, :, 0, :, pl.ds(pl.multiple_of(rows, 1024), 1024)], write.at[5 * d]
        )

    def copy_1(d, inner):
        where = pl.multiple_of(sum(column(distances[d], inner)), 256)
        return pltpu.make_async_copy(
            held_1.at[d, inner], out.at[:, :, 1, :, pl.ds(where, 256)], write.at[5 * d + 1 + inner]
        )

    copies = []
    for d, distance in enumerate(distances):
        for h in range(2):
            for inner in range(4):
                kx, ky = (inner, distance) if h == 0 else (distance, inner)
                near, far = column(kx, ky)
                where = pl.ds(pl.multiple_of(near + far, 256), 256)
                for side in range(2):
                    ref, row = pick(refs, side, d, h, inner)
                    piece = ref[row : row + 512].reshape(4, 2, 64, 128)
                    wide = jnp.concatenate([piece[:, zh].reshape(256, 128) for zh in range(2)], axis=-1)
                    delta = jnp.dot(blocks[side, h], wide, preferred_element_type=jnp.float32)
                    owner = core if side == 0 else 1 - core
                    old = base[:, owner, h, :, where].astype(jnp.float32)
                    new = (old + 0.125 * delta.reshape(4, 48, 256)).astype(HALF)
                    if h == 0:
                        held_0[d, :, owner, :, pl.ds(pl.multiple_of(near, 256), 256)] = new
                    else:
                        held_1[d, inner, :, owner] = new
                if h == 1:
                    copies.append(copy_1(d, inner))
                    copies[-1].start()
            if h == 0:
                copies.append(copy_0(d))
                copies[-1].start()
    for copy in copies:
        copy.wait()


def next_merge_kernel(place, blocks, base, *refs, **how):
    merge_kernel(place, blocks, base, *refs[:-5], *refs[-4:], **how)


def pick_first(refs, side, d, h, inner):
    return refs[side], 2048 * h + 512 * inner


def pick_near(refs, side, d, h, inner):
    if side == 0:
        return refs[2 * d + h], 512 * inner
    return refs[4], 2048 * (2 * d + h) + 512 * inner


def pick_far(refs, side, d, h, inner):
    return refs[4 * side + 2 * (inner // 2) + h], 512 * (inner % 2)


def hop(value, axis, k):
    n = lax.axis_size(axis)
    return lax.ppermute(value, axis, [(i, i ^ k) for i in range(n)])


def swap(value, axis, mask):
    n = lax.axis_size(axis)
    return lax.ppermute(value, axis, [(i, i ^ mask) for i in range(n)])


def per_device(
    grad_a, grad_b, factor_a, factor_b, moment_a, second_a, moment_b, second_b, base_rows
):
    f32 = jnp.float32
    shape = jax.ShapeDtypeStruct
    sa, sb = shape((2, 64, 128), f32), shape((2, 48, 64), f32)
    needed = (grad_a, grad_b, factor_a, factor_b, moment_a, second_a, moment_b, second_b)
    x, y, core, zl, zh = (lax.axis_index(a).astype(jnp.int32) for a in ("x", "y", "core", "zl", "zh"))
    where = jnp.stack([core, zl])
    keep, give, *state = pl.pallas_call(
        pack_kernel,
        out_shape=[pltpu.VMEM((4, 176, 128), f32), pltpu.VMEM((4, 176, 128), HALF)]
        + [pltpu.VMEM(v.shape, f32) for v in needed[2:]],
        in_specs=[SMEM] + [HBM] * 8,
        out_specs=[VMEM] * 8,
        scratch_shapes=[pltpu.VMEM(v.shape, f32) for v in needed[:2]] + [pltpu.SemaphoreType.DMA((8,))],
        compiler_params=limit(4),
    )(where, *[pltpu.with_memory_space_constraint(v, pltpu.HBM) for v in needed])
    own, *parts = pl.pallas_call(
        pair_sum_kernel,
        out_shape=[pltpu.VMEM((176, 128), f32)] + [pltpu.VMEM((176, 128), HALF)] * 3,
        in_specs=[SMEM] + [VMEM] * 2,
        out_specs=[VMEM] * 4,
        compiler_params=limit(4),
    )(where, inside(keep), inside(hop(give, "core", 1)))
    parts = [hop(v, "zl", a) for a, v in enumerate(parts, 1)]
    parts = lax.optimization_barrier(parts)
    state = [inside(v) for v in state]
    send, send_a, total = pl.pallas_call(
        send_kernel,
        out_shape=(pltpu.VMEM((176, 128), HALF), pltpu.VMEM((128, 128), HALF), pltpu.VMEM((176, 128), f32)),
        in_specs=[VMEM] * 10,
        out_specs=(VMEM,) * 3,
        compiler_params=limit(4),
    )(inside(own), *[inside(v) for v in parts], *state)
    pair = pl.pallas_call(
        pair_kernel,
        out_shape=pltpu.VMEM((304, 128), HALF),
        in_specs=[VMEM] * 2,
        out_specs=VMEM,
        compiler_params=limit(2),
    )(inside(send), inside(hop(send_a, "zh", 1)))
    line = [pair] + [hop(pair, "zl", a) for a in (1, 2, 3)]
    line = lax.optimization_barrier(line)

    half_0, half_1, rows_own = pl.pallas_call(
        split_kernel,
        out_shape=(pltpu.VMEM((8, 64, 128), HALF),) * 2 + (pltpu.VMEM((4, 48, 128), HALF),),
        in_specs=[SMEM] + [VMEM] * 4,
        out_specs=(VMEM,) * 3,
        compiler_params=limit(4),
    )(jnp.stack([zl, zh]), *[inside(v) for v in line])
    half_0, half_1 = half_0.reshape(512, 128), half_1.reshape(512, 128)
    halves = half_0, half_1

    first, second = ("x", "y"), ("y", "x")
    parts = [[halves[h]] + [hop(halves[h], first[h], k) for k in (1, 2, 3)] for h in range(2)]
    parts = lax.optimization_barrier(parts)
    mine_0, mine_1, everything = pl.pallas_call(
        join_kernel,
        out_shape=(pltpu.VMEM((2048, 128), HALF),) * 2 + (pltpu.VMEM((4288, 128), HALF),),
        in_specs=[VMEM] * 9,
        out_specs=(VMEM,) * 3,
        compiler_params=limit(6),
    )(*[inside(p) for p in parts[0] + parts[1]], inside(rows_own))
    mine = mine_0, mine_1
    near = [hop(mine[h], second[h], k) for k in (1, 3) for h in range(2)]
    other = hop(everything, "core", 1)
    base, mine_0 = lax.optimization_barrier((base_rows, mine_0))
    base = pl.pallas_call(
        stash_kernel,
        out_shape=pltpu.VMEM((4, 2, 2, 48, 4096), HALF),
        in_specs=[HBM],
        out_specs=VMEM,
        scratch_shapes=[pltpu.SemaphoreType.DMA((4,))],
        compiler_params=limit(2),
        cost_estimate=cost(1024),
    )(pltpu.with_memory_space_constraint(base.reshape(4, 2, 2, 48, 4096), pltpu.HBM))
    blocks = pl.pallas_call(
        blocks_kernel,
        out_shape=pltpu.VMEM((2, 2, 192, 256), HALF),
        in_specs=[VMEM] * 2,
        out_specs=VMEM,
        compiler_params=limit(4),
    )(inside(rows_own), inside(other))
    states = pl.pallas_call(
        state_kernel,
        out_shape=(sa, sb, sa, sa, sb, sb),
        in_specs=[VMEM] + [HBM] * 6,
        out_specs=[VMEM] * 6,
        scratch_shapes=[pltpu.VMEM(v.shape, f32) for v in needed[2:]] + [pltpu.SemaphoreType.DMA((6,))],
        compiler_params=limit(4),
        cost_estimate=cost(1024),
    )(inside(total), *[pltpu.with_memory_space_constraint(v, pltpu.HBM) for v in needed[2:]])

    place = jnp.stack([x, y, core])

    def merge(distances, pick, pieces, before):
        n = len(distances)
        before = [] if before is None else [before]
        return pl.pallas_call(
            functools.partial(next_merge_kernel if before else merge_kernel, distances=distances, pick=pick),
            out_shape=shape((4, 2, 2, 48, 4096), HALF),
            in_specs=[SMEM, VMEM, VMEM] + [VMEM] * len(pieces) + [HBM] * len(before),
            out_specs=HBM,
            input_output_aliases={3 + len(pieces): 0} if before else {},
            scratch_shapes=[
                pltpu.VMEM((n, 4, 2, 48, 1024), HALF),
                pltpu.VMEM((n, 4, 4, 2, 48, 256), HALF),
                pltpu.SemaphoreType.DMA((5 * n,)),
            ],
            compiler_params=limit(2 + 2 * n),
            cost_estimate=cost(1024),
        )(place, inside(blocks), inside(base), *[inside(v) for v in pieces], *before)

    merged = merge((0,), pick_first, [everything, other], None)
    near, merged, states = lax.optimization_barrier((near, merged, states))
    half = shape((1024, 128), HALF)
    *relayed, everything = pl.pallas_call(
        relay_kernel,
        out_shape=(half,) * 4 + (shape((8192, 128), HALF),),
        in_specs=[VMEM] * 4,
        out_specs=(VMEM,) * 5,
        compiler_params=limit(8),
    )(*near)
    far = [hop(relayed[2 * s + h], second[h], 3 - 2 * s) for s in range(2) for h in range(2)]
    near_other = hop(everything, "core", 1)
    merged = merge((1, 3), pick_near, [*near, near_other], merged)
    far, merged = lax.optimization_barrier((far, merged))
    far_other = [hop(v, "core", 1) for v in far]
    merged = merge((2,), pick_far, far + far_other, merged)
    new_a, new_b, new_ma, new_va, new_mb, new_vb = states
    return (new_a, new_b, new_ma, new_va, new_mb, new_vb, merged.reshape(16, 48, 4096))


def solution(mesh):
    fine = Mesh(mesh.devices.reshape(4, 2, 4, 4, 2), ("zl", "core", "y", "x", "zh"))
    group, tensor = ("zl", "core"), ("y", "x", "zh")
    in_specs = (
        P(group, None, None, tensor),
        P(group, None, tensor, None),
        P(group, None, tensor),
        P(group, tensor, None),
        P(group, None, tensor),
        P(group, None, tensor),
        P(group, tensor, None),
        P(group, tensor, None),
        P(None, tensor, None),
    )
    out_specs = (
        P(group, None, tensor),
        P(group, tensor, None),
        P(group, None, tensor),
        P(group, None, tensor),
        P(group, tensor, None),
        P(group, tensor, None),
        P(None, tensor, None),
    )
    return jax.shard_map(
        per_device, mesh=fine, in_specs=in_specs, out_specs=out_specs, check_vma=False
    )
```

```python
import functools

import jax
import jax.numpy as jnp
from jax import lax
from jax.experimental import pallas as pl
from jax.experimental.pallas import tpu as pltpu
from jax.sharding import Mesh, PartitionSpec as P

STEP = 100
HALF = jnp.bfloat16
VMEM = pl.BlockSpec(memory_space=pltpu.VMEM)
SMEM = pl.BlockSpec(memory_space=pltpu.SMEM)
HBM = pl.BlockSpec(memory_space=pltpu.HBM)


def cost(size):
    return pl.CostEstimate(flops=0, bytes_accessed=size, transcendentals=0)


def limit(size):
    return pltpu.CompilerParams(vmem_limit_bytes=size * 2**20)


def inside(value):
    return pltpu.with_memory_space_constraint(value, pltpu.VMEM)


def adam_update(param, grad, first, second):
    new_first = 0.9 * first + 0.1 * grad
    new_second = 0.999 * second + 0.001 * grad * grad
    corr_first = new_first / (1.0 - 0.9**STEP)
    corr_second = new_second / (1.0 - 0.999**STEP)
    new_param = param - 0.1 * corr_first / (jnp.sqrt(corr_second) + 1e-08)
    return (new_param, new_first, new_second)


def fetched(there, here, sems):
    copies = [pltpu.make_async_copy(t, h, sems.at[i]) for i, (t, h) in enumerate(zip(there, here))]
    for copy in copies:
        copy.start()
    return copies


def pack_kernel(place, *refs):
    there, (keep, give), here = refs[:8], refs[8:10], refs[10:16]
    grad_a, grad_b, sems = refs[16:]
    copies = fetched(there, (grad_a, grad_b, *here), sems)
    copies[0].wait()
    copies[1].wait()
    core = place[0]
    for out, owner_core in ((keep, core), (give, 1 - core)):
        for zl in range(4):
            expert = 4 * zl + 2 * owner_core
            out[zl, 0:128] = grad_a[0, pl.ds(expert, 2)].reshape(128, 128).astype(out.dtype)
            both = jnp.concatenate([grad_b[0, expert], grad_b[0, expert + 1]], axis=-1)
            out[zl, 128:176] = both.astype(out.dtype)
    for copy in copies[2:]:
        copy.wait()


def pair_sum_kernel(place, keep, given, own, out_1, out_2, out_3):
    zl = place[1]
    own[...] = keep[zl] + given[zl].astype(jnp.float32)
    for a, out in ((1, out_1), (2, out_2), (3, out_3)):
        out[...] = (keep[zl ^ a] + given[zl ^ a].astype(jnp.float32)).astype(HALF)


def apart(total):
    return total[0:128].reshape(2, 64, 128), [total[128:176, 64 * e : 64 * e + 64] for e in range(2)]


def send_kernel(
    own, got_1, got_2, got_3, factor_a, factor_b, moment_a, second_a, moment_b, second_b, send, send_a, total
):
    total[...] = own[...] + (got_1[...].astype(jnp.float32) + (got_2[...].astype(jnp.float32) + got_3[...].astype(jnp.float32)))
    grad_a, grad_b = apart(total)
    a = adam_update(factor_a[...], grad_a, moment_a[...], second_a[...])[0]
    b = [adam_update(factor_b[e], grad_b[e], moment_b[e], second_b[e])[0] for e in range(2)]
    a_half = a.astype(HALF).reshape(128, 128)
    b_half = jnp.concatenate(b, axis=-1).astype(HALF)
    send[0:128] = a_half
    send[128:176] = b_half
    send_a[...] = a_half


def state_kernel(total, *refs):
    there, (new_a, new_b, new_ma, new_va, new_mb, new_vb) = refs[:6], refs[6:12]
    here, sems = refs[12:18], refs[18]
    for copy in fetched(there, here, sems):
        copy.wait()
    factor_a, factor_b, moment_a, second_a, moment_b, second_b = here
    grad_a, grad_b = apart(total)
    new_a[...], new_ma[...], new_va[...] = adam_update(
        factor_a[...], grad_a, moment_a[...], second_a[...]
    )
    for e in range(2):
        new_b[e], new_mb[e], new_vb[e] = adam_update(
            factor_b[e], grad_b[e], moment_b[e], second_b[e]
        )


def pair_kernel(send, across, pair):
    pair[0:128] = send[0:128]
    pair[128:256] = across[...]
    pair[256:304] = send[128:176]


def split_kernel(place, *refs):
    half_0, half_1, rows = refs[4:]
    zl, zh = place[0], place[1]
    for a in range(4):
        for b in range(2):
            slot = (zl ^ a) * 2 + (zh ^ b)
            half_0[slot] = refs[a][128 * b : 128 * b + 64]
            half_1[slot] = refs[a][128 * b + 64 : 128 * b + 128]
        rows[zl ^ a] = refs[a][256:304]


def join_kernel(*refs):
    for h in range(2):
        for k in range(4):
            refs[8 + h][512 * k : 512 * k + 512] = refs[4 * h + k][...]


def blocks_kernel(rows_own, other, blocks):
    rows_sibling = other[...]
    for side, rows in ((0, rows_own[...]), (1, rows_sibling)):
        for h in range(2):
            for zl in range(4):
                parts = []
                if zl:
                    parts.append(jnp.zeros((48, 64 * zl), HALF))
                parts.append(rows[zl, :, 64 * h : 64 * h + 64])
                if zl < 3:
                    parts.append(jnp.zeros((48, 192 - 64 * zl), HALF))
                blocks[side, h, 48 * zl : 48 * zl + 48, :] = jnp.concatenate(parts, axis=-1)


def relay_kernel(up_0, up_1, down_0, down_1, half_0, half_1, half_2, half_3, everything):
    half_0[...] = up_0[0:1024]
    half_1[...] = up_1[0:1024]
    half_2[...] = down_0[1024:2048]
    half_3[...] = down_1[1024:2048]
    for k, piece in enumerate((up_0, up_1, down_0, down_1)):
        everything[2048 * k : 2048 * k + 2048] = piece[...]


def stash_kernel(base, kept, sems):
    for copy in fetched([base.at[zl] for zl in range(4)], [kept.at[zl] for zl in range(4)], sems):
        copy.wait()


def merge_kernel(place, blocks, base, *refs, distances, pick):
    out, held_0, held_1, write = refs[-4:]
    x, y, core = place[0], place[1], place[2]

    def column(kx, ky):
        return (x ^ kx) * 256, (y ^ ky) * 1024

    def copy_0(d):
        rows = column(0, distances[d])[1]
        return pltpu.make_async_copy(
            held_0.at[d], out.at[:, :, 0, :, pl.ds(pl.multiple_of(rows, 1024), 1024)], write.at[5 * d]
        )

    def copy_1(d, inner):
        where = pl.multiple_of(sum(column(distances[d], inner)), 256)
        return pltpu.make_async_copy(
            held_1.at[d, inner], out.at[:, :, 1, :, pl.ds(where, 256)], write.at[5 * d + 1 + inner]
        )

    copies = []
    for d, distance in enumerate(distances):
        for h in range(2):
            for inner in range(4):
                kx, ky = (inner, distance) if h == 0 else (distance, inner)
                near, far = column(kx, ky)
                where = pl.ds(pl.multiple_of(near + far, 256), 256)
                for side in range(2):
                    ref, row = pick(refs, side, d, h, inner)
                    piece = ref[row : row + 512].reshape(4, 2, 64, 128)
                    wide = jnp.concatenate([piece[:, zh].reshape(256, 128) for zh in range(2)], axis=-1)
                    delta = jnp.dot(blocks[side, h], wide, preferred_element_type=jnp.float32)
                    owner = core if side == 0 else 1 - core
                    old = base[:, owner, h, :, where].astype(jnp.float32)
                    new = (old + 0.125 * delta.reshape(4, 48, 256)).astype(HALF)
                    if h == 0:
                        held_0[d, :, owner, :, pl.ds(pl.multiple_of(near, 256), 256)] = new
                    else:
                        held_1[d, inner, :, owner] = new
                if h == 1:
                    copies.append(copy_1(d, inner))
                    copies[-1].start()
            if h == 0:
                copies.append(copy_0(d))
                copies[-1].start()
    for copy in copies:
        copy.wait()


def next_merge_kernel(place, blocks, base, *refs, **how):
    merge_kernel(place, blocks, base, *refs[:-5], *refs[-4:], **how)


def pick_first(refs, side, d, h, inner):
    return refs[2 * side + h], 512 * inner


def pick_near(refs, side, d, h, inner):
    if side == 0:
        return refs[2 * d + h], 512 * inner
    return refs[4], 2048 * (2 * d + h) + 512 * inner


def pick_far(refs, side, d, h, inner):
    return refs[4 * side + 2 * (inner // 2) + h], 512 * (inner % 2)


def hop(value, axis, k):
    n = lax.axis_size(axis)
    return lax.ppermute(value, axis, [(i, i ^ k) for i in range(n)])


def swap(value, axis, mask):
    n = lax.axis_size(axis)
    return lax.ppermute(value, axis, [(i, i ^ mask) for i in range(n)])


def per_device(
    grad_a, grad_b, factor_a, factor_b, moment_a, second_a, moment_b, second_b, base_rows
):
    f32 = jnp.float32
    shape = jax.ShapeDtypeStruct
    sa, sb = shape((2, 64, 128), f32), shape((2, 48, 64), f32)
    needed = (grad_a, grad_b, factor_a, factor_b, moment_a, second_a, moment_b, second_b)
    x, y, core, zl, zh = (lax.axis_index(a).astype(jnp.int32) for a in ("x", "y", "core", "zl", "zh"))
    where = jnp.stack([core, zl])
    keep, give, *state = pl.pallas_call(
        pack_kernel,
        out_shape=[pltpu.VMEM((4, 176, 128), f32), pltpu.VMEM((4, 176, 128), HALF)]
        + [pltpu.VMEM(v.shape, f32) for v in needed[2:]],
        in_specs=[SMEM] + [HBM] * 8,
        out_specs=[VMEM] * 8,
        scratch_shapes=[pltpu.VMEM(v.shape, f32) for v in needed[:2]] + [pltpu.SemaphoreType.DMA((8,))],
        compiler_params=limit(4),
    )(where, *[pltpu.with_memory_space_constraint(v, pltpu.HBM) for v in needed])
    own, *parts = pl.pallas_call(
        pair_sum_kernel,
        out_shape=[pltpu.VMEM((176, 128), f32)] + [pltpu.VMEM((176, 128), HALF)] * 3,
        in_specs=[SMEM] + [VMEM] * 2,
        out_specs=[VMEM] * 4,
        compiler_params=limit(4),
    )(where, inside(keep), inside(hop(give, "core", 1)))
    parts = [hop(v, "zl", a) for a, v in enumerate(parts, 1)]
    parts = lax.optimization_barrier(parts)
    state = [inside(v) for v in state]
    send, send_a, total = pl.pallas_call(
        send_kernel,
        out_shape=(pltpu.VMEM((176, 128), HALF), pltpu.VMEM((128, 128), HALF), pltpu.VMEM((176, 128), f32)),
        in_specs=[VMEM] * 10,
        out_specs=(VMEM,) * 3,
        compiler_params=limit(4),
    )(inside(own), *[inside(v) for v in parts], *state)
    pair = pl.pallas_call(
        pair_kernel,
        out_shape=pltpu.VMEM((304, 128), HALF),
        in_specs=[VMEM] * 2,
        out_specs=VMEM,
        compiler_params=limit(2),
    )(inside(send), inside(hop(send_a, "zh", 1)))
    line = [pair] + [hop(pair, "zl", a) for a in (1, 2, 3)]
    line = lax.optimization_barrier(line)

    half_0, half_1, rows_own = pl.pallas_call(
        split_kernel,
        out_shape=(pltpu.VMEM((8, 64, 128), HALF),) * 2 + (pltpu.VMEM((4, 48, 128), HALF),),
        in_specs=[SMEM] + [VMEM] * 4,
        out_specs=(VMEM,) * 3,
        compiler_params=limit(4),
    )(jnp.stack([zl, zh]), *[inside(v) for v in line])
    half_0, half_1 = half_0.reshape(512, 128), half_1.reshape(512, 128)
    halves = half_0, half_1

    first, second = ("x", "y"), ("y", "x")
    pieces = {(h, k): hop(halves[h], first[h], k) for k in (1, 3, 2) for h in range(2)}
    pieces = lax.optimization_barrier([pieces[h, k] for k in (1, 3, 2) for h in range(2)])
    parts = [[halves[h], pieces[h], pieces[4 + h], pieces[2 + h]] for h in range(2)]
    mine_0, mine_1 = pl.pallas_call(
        join_kernel,
        out_shape=(pltpu.VMEM((2048, 128), HALF),) * 2,
        in_specs=[VMEM] * 8,
        out_specs=(VMEM,) * 2,
        compiler_params=limit(4),
    )(*[inside(p) for p in parts[0] + parts[1]])
    mine = mine_0, mine_1
    near = [hop(mine[h], second[h], k) for k in (1, 3) for h in range(2)]
    other = [hop(v, "core", 1) for v in mine]
    rows_other = hop(rows_own, "core", 1)
    base, mine_0 = lax.optimization_barrier((base_rows, mine_0))
    base = pl.pallas_call(
        stash_kernel,
        out_shape=pltpu.VMEM((4, 2, 2, 48, 4096), HALF),
        in_specs=[HBM],
        out_specs=VMEM,
        scratch_shapes=[pltpu.SemaphoreType.DMA((4,))],
        compiler_params=limit(2),
        cost_estimate=cost(1024),
    )(pltpu.with_memory_space_constraint(base.reshape(4, 2, 2, 48, 4096), pltpu.HBM))
    blocks = pl.pallas_call(
        blocks_kernel,
        out_shape=pltpu.VMEM((2, 2, 192, 256), HALF),
        in_specs=[VMEM] * 2,
        out_specs=VMEM,
        compiler_params=limit(4),
    )(inside(rows_own), inside(rows_other))
    states = pl.pallas_call(
        state_kernel,
        out_shape=(sa, sb, sa, sa, sb, sb),
        in_specs=[VMEM] + [HBM] * 6,
        out_specs=[VMEM] * 6,
        scratch_shapes=[pltpu.VMEM(v.shape, f32) for v in needed[2:]] + [pltpu.SemaphoreType.DMA((6,))],
        compiler_params=limit(4),
        cost_estimate=cost(1024),
    )(inside(total), *[pltpu.with_memory_space_constraint(v, pltpu.HBM) for v in needed[2:]])

    place = jnp.stack([x, y, core])

    def merge(distances, pick, pieces, before):
        n = len(distances)
        before = [] if before is None else [before]
        return pl.pallas_call(
            functools.partial(next_merge_kernel if before else merge_kernel, distances=distances, pick=pick),
            out_shape=shape((4, 2, 2, 48, 4096), HALF),
            in_specs=[SMEM, VMEM, VMEM] + [VMEM] * len(pieces) + [HBM] * len(before),
            out_specs=HBM,
            input_output_aliases={3 + len(pieces): 0} if before else {},
            scratch_shapes=[
                pltpu.VMEM((n, 4, 2, 48, 1024), HALF),
                pltpu.VMEM((n, 4, 4, 2, 48, 256), HALF),
                pltpu.SemaphoreType.DMA((5 * n,)),
            ],
            compiler_params=limit(2 + 2 * n),
            cost_estimate=cost(1024),
        )(place, inside(blocks), inside(base), *[inside(v) for v in pieces], *before)

    merged = merge((0,), pick_first, [*mine, *other], None)
    near, merged, states = lax.optimization_barrier((near, merged, states))
    half = shape((1024, 128), HALF)
    *relayed, everything = pl.pallas_call(
        relay_kernel,
        out_shape=(half,) * 4 + (shape((8192, 128), HALF),),
        in_specs=[VMEM] * 4,
        out_specs=(VMEM,) * 5,
        compiler_params=limit(8),
    )(*near)
    far = [hop(relayed[2 * s + h], second[h], 3 - 2 * s) for s in range(2) for h in range(2)]
    near_other = hop(everything, "core", 1)
    merged = merge((1, 3), pick_near, [*near, near_other], merged)
    far, merged = lax.optimization_barrier((far, merged))
    far_other = [hop(v, "core", 1) for v in far]
    merged = merge((2,), pick_far, far + far_other, merged)
    new_a, new_b, new_ma, new_va, new_mb, new_vb = states
    return (new_a, new_b, new_ma, new_va, new_mb, new_vb, merged.reshape(16, 48, 4096))


def solution(mesh):
    fine = Mesh(mesh.devices.reshape(4, 2, 4, 4, 2), ("zl", "core", "y", "x", "zh"))
    group, tensor = ("zl", "core"), ("y", "x", "zh")
    in_specs = (
        P(group, None, None, tensor),
        P(group, None, tensor, None),
        P(group, None, tensor),
        P(group, tensor, None),
        P(group, None, tensor),
        P(group, None, tensor),
        P(group, tensor, None),
        P(group, tensor, None),
        P(None, tensor, None),
    )
    out_specs = (
        P(group, None, tensor),
        P(group, tensor, None),
        P(group, None, tensor),
        P(group, None, tensor),
        P(group, tensor, None),
        P(group, tensor, None),
        P(None, tensor, None),
    )
    return jax.shard_map(
        per_device, mesh=fine, in_specs=in_specs, out_specs=out_specs, check_vma=False
    )
```

```python
import functools

import jax
import jax.numpy as jnp
from jax import lax
from jax.experimental import pallas as pl
from jax.experimental.pallas import tpu as pltpu
from jax.sharding import Mesh, PartitionSpec as P

STEP = 100
HALF = jnp.bfloat16
VMEM = pl.BlockSpec(memory_space=pltpu.VMEM)
SMEM = pl.BlockSpec(memory_space=pltpu.SMEM)
HBM = pl.BlockSpec(memory_space=pltpu.HBM)


def cost(size):
    return pl.CostEstimate(flops=0, bytes_accessed=size, transcendentals=0)


def limit(size):
    return pltpu.CompilerParams(vmem_limit_bytes=size * 2**20)


def inside(value):
    return pltpu.with_memory_space_constraint(value, pltpu.VMEM)


def adam_update(param, grad, first, second):
    new_first = 0.9 * first + 0.1 * grad
    new_second = 0.999 * second + 0.001 * grad * grad
    corr_first = new_first / (1.0 - 0.9**STEP)
    corr_second = new_second / (1.0 - 0.999**STEP)
    new_param = param - 0.1 * corr_first / (jnp.sqrt(corr_second) + 1e-08)
    return (new_param, new_first, new_second)


def fetched(there, here, sems):
    copies = [pltpu.make_async_copy(t, h, sems.at[i]) for i, (t, h) in enumerate(zip(there, here))]
    for copy in copies:
        copy.start()
    return copies


def pack_kernel(place, *refs):
    there, (keep, give), here = refs[:8], refs[8:10], refs[10:16]
    grad_a, grad_b, sems = refs[16:]
    copies = fetched(there, (grad_a, grad_b, *here), sems)
    copies[0].wait()
    copies[1].wait()
    core = place[0]
    for out, owner_core in ((keep, core), (give, 1 - core)):
        for zl in range(4):
            expert = 4 * zl + 2 * owner_core
            out[zl, 0:128] = grad_a[0, pl.ds(expert, 2)].reshape(128, 128).astype(out.dtype)
            both = jnp.concatenate([grad_b[0, expert], grad_b[0, expert + 1]], axis=-1)
            out[zl, 128:176] = both.astype(out.dtype)
    for copy in copies[2:]:
        copy.wait()


def pair_sum_kernel(place, keep, given, own, out_1, out_2, out_3):
    zl = place[1]
    own[...] = keep[zl] + given[zl].astype(jnp.float32)
    for a, out in ((1, out_1), (2, out_2), (3, out_3)):
        out[...] = (keep[zl ^ a] + given[zl ^ a].astype(jnp.float32)).astype(HALF)


def apart(total):
    return total[0:128].reshape(2, 64, 128), [total[128:176, 64 * e : 64 * e + 64] for e in range(2)]


def send_kernel(
    own, got_1, got_2, got_3, factor_a, factor_b, moment_a, second_a, moment_b, second_b, send, send_a, total
):
    total[...] = own[...] + (got_1[...].astype(jnp.float32) + (got_2[...].astype(jnp.float32) + got_3[...].astype(jnp.float32)))
    grad_a, grad_b = apart(total)
    a = adam_update(factor_a[...], grad_a, moment_a[...], second_a[...])[0]
    b = [adam_update(factor_b[e], grad_b[e], moment_b[e], second_b[e])[0] for e in range(2)]
    a_half = a.astype(HALF).reshape(128, 128)
    b_half = jnp.concatenate(b, axis=-1).astype(HALF)
    send[0:128] = a_half
    send[128:176] = b_half
    send_a[...] = a_half


def state_kernel(total, *refs):
    there, (new_a, new_b, new_ma, new_va, new_mb, new_vb) = refs[:6], refs[6:12]
    here, sems = refs[12:18], refs[18]
    for copy in fetched(there, here, sems):
        copy.wait()
    factor_a, factor_b, moment_a, second_a, moment_b, second_b = here
    grad_a, grad_b = apart(total)
    new_a[...], new_ma[...], new_va[...] = adam_update(
        factor_a[...], grad_a, moment_a[...], second_a[...]
    )
    for e in range(2):
        new_b[e], new_mb[e], new_vb[e] = adam_update(
            factor_b[e], grad_b[e], moment_b[e], second_b[e]
        )


def pair_kernel(send, across, pair):
    pair[0:128] = send[0:128]
    pair[128:256] = across[...]
    pair[256:304] = send[128:176]


def split_kernel(place, *refs):
    half_0, half_1, rows = refs[4:]
    zl, zh = place[0], place[1]
    for a in range(4):
        for b in range(2):
            slot = (zl ^ a) * 2 + (zh ^ b)
            half_0[slot] = refs[a][128 * b : 128 * b + 64]
            half_1[slot] = refs[a][128 * b + 64 : 128 * b + 128]
        rows[zl ^ a] = refs[a][256:304]


def join_kernel(*refs):
    for h in range(2):
        for k in range(4):
            refs[8 + h][512 * k : 512 * k + 512] = refs[4 * h + k][...]


def blocks_kernel(rows_own, other, blocks):
    rows_sibling = other[...]
    for side, rows in ((0, rows_own[...]), (1, rows_sibling)):
        for h in range(2):
            for zl in range(4):
                parts = []
                if zl:
                    parts.append(jnp.zeros((48, 64 * zl), HALF))
                parts.append(rows[zl, :, 64 * h : 64 * h + 64])
                if zl < 3:
                    parts.append(jnp.zeros((48, 192 - 64 * zl), HALF))
                blocks[side, h, 48 * zl : 48 * zl + 48, :] = jnp.concatenate(parts, axis=-1)


def relay_kernel(up_0, up_1, down_0, down_1, half_0, half_1, half_2, half_3):
    half_0[...] = up_0[0:1024]
    half_1[...] = up_1[0:1024]
    half_2[...] = down_0[1024:2048]
    half_3[...] = down_1[1024:2048]


def stash_kernel(base, kept, sems):
    for copy in fetched([base.at[zl] for zl in range(4)], [kept.at[zl] for zl in range(4)], sems):
        copy.wait()


def merge_kernel(place, blocks, base, *refs, distances, pick):
    out, held_0, held_1, write = refs[-4:]
    x, y, core = place[0], place[1], place[2]

    def column(kx, ky):
        return (x ^ kx) * 256, (y ^ ky) * 1024

    def copy_0(d):
        rows = column(0, distances[d])[1]
        return pltpu.make_async_copy(
            held_0.at[d], out.at[:, :, 0, :, pl.ds(pl.multiple_of(rows, 1024), 1024)], write.at[5 * d]
        )

    def copy_1(d, inner):
        where = pl.multiple_of(sum(column(distances[d], inner)), 256)
        return pltpu.make_async_copy(
            held_1.at[d, inner], out.at[:, :, 1, :, pl.ds(where, 256)], write.at[5 * d + 1 + inner]
        )

    copies = []
    for d, distance in enumerate(distances):
        for h in range(2):
            for inner in range(4):
                kx, ky = (inner, distance) if h == 0 else (distance, inner)
                near, far = column(kx, ky)
                where = pl.ds(pl.multiple_of(near + far, 256), 256)
                for side in range(2):
                    ref, row = pick(refs, side, d, h, inner)
                    piece = ref[row : row + 512].reshape(4, 2, 64, 128)
                    wide = jnp.concatenate([piece[:, zh].reshape(256, 128) for zh in range(2)], axis=-1)
                    delta = jnp.dot(blocks[side, h], wide, preferred_element_type=jnp.float32)
                    owner = core if side == 0 else 1 - core
                    old = base[:, owner, h, :, where].astype(jnp.float32)
                    new = (old + 0.125 * delta.reshape(4, 48, 256)).astype(HALF)
                    if h == 0:
                        held_0[d, :, owner, :, pl.ds(pl.multiple_of(near, 256), 256)] = new
                    else:
                        held_1[d, inner, :, owner] = new
                if h == 1:
                    copies.append(copy_1(d, inner))
                    copies[-1].start()
            if h == 0:
                copies.append(copy_0(d))
                copies[-1].start()
    for copy in copies:
        copy.wait()


def next_merge_kernel(place, blocks, base, *refs, **how):
    merge_kernel(place, blocks, base, *refs[:-5], *refs[-4:], **how)


def pick_first(refs, side, d, h, inner):
    return refs[2 * side + h], 512 * inner


def pick_near(refs, side, d, h, inner):
    if side == 0:
        return refs[2 * d + h], 512 * inner
    return refs[4 + 2 * d + h], 512 * inner


def pick_far(refs, side, d, h, inner):
    return refs[4 * side + 2 * (inner // 2) + h], 512 * (inner % 2)


def hop(value, axis, k):
    n = lax.axis_size(axis)
    return lax.ppermute(value, axis, [(i, i ^ k) for i in range(n)])


def swap(value, axis, mask):
    n = lax.axis_size(axis)
    return lax.ppermute(value, axis, [(i, i ^ mask) for i in range(n)])


def per_device(
    grad_a, grad_b, factor_a, factor_b, moment_a, second_a, moment_b, second_b, base_rows
):
    f32 = jnp.float32
    shape = jax.ShapeDtypeStruct
    sa, sb = shape((2, 64, 128), f32), shape((2, 48, 64), f32)
    needed = (grad_a, grad_b, factor_a, factor_b, moment_a, second_a, moment_b, second_b)
    x, y, core, zl, zh = (lax.axis_index(a).astype(jnp.int32) for a in ("x", "y", "core", "zl", "zh"))
    where = jnp.stack([core, zl])
    keep, give, *state = pl.pallas_call(
        pack_kernel,
        out_shape=[pltpu.VMEM((4, 176, 128), f32), pltpu.VMEM((4, 176, 128), HALF)]
        + [pltpu.VMEM(v.shape, f32) for v in needed[2:]],
        in_specs=[SMEM] + [HBM] * 8,
        out_specs=[VMEM] * 8,
        scratch_shapes=[pltpu.VMEM(v.shape, f32) for v in needed[:2]] + [pltpu.SemaphoreType.DMA((8,))],
        compiler_params=limit(4),
    )(where, *[pltpu.with_memory_space_constraint(v, pltpu.HBM) for v in needed])
    own, *parts = pl.pallas_call(
        pair_sum_kernel,
        out_shape=[pltpu.VMEM((176, 128), f32)] + [pltpu.VMEM((176, 128), HALF)] * 3,
        in_specs=[SMEM] + [VMEM] * 2,
        out_specs=[VMEM] * 4,
        compiler_params=limit(4),
    )(where, inside(keep), inside(hop(give, "core", 1)))
    parts = [hop(v, "zl", a) for a, v in enumerate(parts, 1)]
    parts = lax.optimization_barrier(parts)
    state = [inside(v) for v in state]
    send, send_a, total = pl.pallas_call(
        send_kernel,
        out_shape=(pltpu.VMEM((176, 128), HALF), pltpu.VMEM((128, 128), HALF), pltpu.VMEM((176, 128), f32)),
        in_specs=[VMEM] * 10,
        out_specs=(VMEM,) * 3,
        compiler_params=limit(4),
    )(inside(own), *[inside(v) for v in parts], *state)
    pair = pl.pallas_call(
        pair_kernel,
        out_shape=pltpu.VMEM((304, 128), HALF),
        in_specs=[VMEM] * 2,
        out_specs=VMEM,
        compiler_params=limit(2),
    )(inside(send), inside(hop(send_a, "zh", 1)))
    line = [pair] + [hop(pair, "zl", a) for a in (1, 2, 3)]
    line = lax.optimization_barrier(line)

    half_0, half_1, rows_own = pl.pallas_call(
        split_kernel,
        out_shape=(pltpu.VMEM((8, 64, 128), HALF),) * 2 + (pltpu.VMEM((4, 48, 128), HALF),),
        in_specs=[SMEM] + [VMEM] * 4,
        out_specs=(VMEM,) * 3,
        compiler_params=limit(4),
    )(jnp.stack([zl, zh]), *[inside(v) for v in line])
    half_0, half_1 = half_0.reshape(512, 128), half_1.reshape(512, 128)
    halves = half_0, half_1

    first, second = ("x", "y"), ("y", "x")
    pieces = {(h, k): hop(halves[h], first[h], k) for k in (1, 3, 2) for h in range(2)}
    pieces = lax.optimization_barrier([pieces[h, k] for k in (1, 3, 2) for h in range(2)])
    parts = [[halves[h], pieces[h], pieces[4 + h], pieces[2 + h]] for h in range(2)]
    mine_0, mine_1 = pl.pallas_call(
        join_kernel,
        out_shape=(pltpu.VMEM((2048, 128), HALF),) * 2,
        in_specs=[VMEM] * 8,
        out_specs=(VMEM,) * 2,
        compiler_params=limit(4),
    )(*[inside(p) for p in parts[0] + parts[1]])
    mine = mine_0, mine_1
    near = [hop(mine[h], second[h], k) for k in (1, 3) for h in range(2)]
    other = [hop(v, "core", 1) for v in mine]
    rows_other = hop(rows_own, "core", 1)
    base, mine_0 = lax.optimization_barrier((base_rows, mine_0))
    base = pl.pallas_call(
        stash_kernel,
        out_shape=pltpu.VMEM((4, 2, 2, 48, 4096), HALF),
        in_specs=[HBM],
        out_specs=VMEM,
        scratch_shapes=[pltpu.SemaphoreType.DMA((4,))],
        compiler_params=limit(2),
        cost_estimate=cost(1024),
    )(pltpu.with_memory_space_constraint(base.reshape(4, 2, 2, 48, 4096), pltpu.HBM))
    blocks = pl.pallas_call(
        blocks_kernel,
        out_shape=pltpu.VMEM((2, 2, 192, 256), HALF),
        in_specs=[VMEM] * 2,
        out_specs=VMEM,
        compiler_params=limit(4),
    )(inside(rows_own), inside(rows_other))
    states = pl.pallas_call(
        state_kernel,
        out_shape=(sa, sb, sa, sa, sb, sb),
        in_specs=[VMEM] + [HBM] * 6,
        out_specs=[VMEM] * 6,
        scratch_shapes=[pltpu.VMEM(v.shape, f32) for v in needed[2:]] + [pltpu.SemaphoreType.DMA((6,))],
        compiler_params=limit(4),
        cost_estimate=cost(1024),
    )(inside(total), *[pltpu.with_memory_space_constraint(v, pltpu.HBM) for v in needed[2:]])

    place = jnp.stack([x, y, core])

    def merge(distances, pick, pieces, before):
        n = len(distances)
        before = [] if before is None else [before]
        return pl.pallas_call(
            functools.partial(next_merge_kernel if before else merge_kernel, distances=distances, pick=pick),
            out_shape=shape((4, 2, 2, 48, 4096), HALF),
            in_specs=[SMEM, VMEM, VMEM] + [VMEM] * len(pieces) + [HBM] * len(before),
            out_specs=HBM,
            input_output_aliases={3 + len(pieces): 0} if before else {},
            scratch_shapes=[
                pltpu.VMEM((n, 4, 2, 48, 1024), HALF),
                pltpu.VMEM((n, 4, 4, 2, 48, 256), HALF),
                pltpu.SemaphoreType.DMA((5 * n,)),
            ],
            compiler_params=limit(2 + 2 * n),
            cost_estimate=cost(1024),
        )(place, inside(blocks), inside(base), *[inside(v) for v in pieces], *before)

    merged = merge((0,), pick_first, [*mine, *other], None)
    near, merged, states = lax.optimization_barrier((near, merged, states))
    half = shape((1024, 128), HALF)
    relayed = pl.pallas_call(
        relay_kernel,
        out_shape=(half,) * 4,
        in_specs=[VMEM] * 4,
        out_specs=(VMEM,) * 4,
        compiler_params=limit(8),
    )(*near)
    far = [hop(relayed[2 * s + h], second[h], 3 - 2 * s) for s in range(2) for h in range(2)]
    near_other = [hop(v, "core", 1) for v in near]
    merged = merge((1, 3), pick_near, [*near, *near_other], merged)
    far, merged = lax.optimization_barrier((far, merged))
    far_other = [hop(v, "core", 1) for v in far]
    merged = merge((2,), pick_far, far + far_other, merged)
    new_a, new_b, new_ma, new_va, new_mb, new_vb = states
    return (new_a, new_b, new_ma, new_va, new_mb, new_vb, merged.reshape(16, 48, 4096))


def solution(mesh):
    fine = Mesh(mesh.devices.reshape(4, 2, 4, 4, 2), ("zl", "core", "y", "x", "zh"))
    group, tensor = ("zl", "core"), ("y", "x", "zh")
    in_specs = (
        P(group, None, None, tensor),
        P(group, None, tensor, None),
        P(group, None, tensor),
        P(group, tensor, None),
        P(group, None, tensor),
        P(group, None, tensor),
        P(group, tensor, None),
        P(group, tensor, None),
        P(None, tensor, None),
    )
    out_specs = (
        P(group, None, tensor),
        P(group, tensor, None),
        P(group, None, tensor),
        P(group, None, tensor),
        P(group, tensor, None),
        P(group, tensor, None),
        P(None, tensor, None),
    )
    return jax.shard_map(
        per_device, mesh=fine, in_specs=in_specs, out_specs=out_specs, check_vma=False
    )
```
